128 devices in a mesh: dp: 16 (over x, y_hi, core), mp: 8 (over y_lo, z).
Axes of the slice: x: 4, y: 4 (y_hi: 2, y_lo: 2; y = y_hi * 2 + y_lo), z: 4, core: 2. Of those that a mesh axis runs over, the one named last changes fastest.
Arguments:
- tokens_in: bfloat16 [16384, 2048], P(('dp', 'mp')), may hold values from -6 to 6
- cotangent: bfloat16 [16384, 2048], P(('dp', 'mp')), may hold values from -6 to 6
- lengths: int32 [16, 3], P('dp'), may hold values from 0 to 1024, as said below
- ln1_gain: float32 [2048], replicated, may hold values from 0.5 to 1.5
- ln1_bias: float32 [2048], replicated, may hold values from -1 to 1
- w_query: bfloat16 [2048, 2048], P(None, 'mp'), may hold values from -0.125 to 0.125
- w_key: bfloat16 [2048, 2048], P(None, 'mp'), may hold values from -0.125 to 0.125
- w_value: bfloat16 [2048, 4096], P(None, 'mp'), may hold values from -0.125 to 0.125
- w_gate: bfloat16 [2048, 4096], P(None, 'mp'), may hold values from -0.125 to 0.125
- w_out: bfloat16 [4096, 2048], P('mp'), may hold values from -0.125 to 0.125
- ln2_gain: float32 [2048], replicated, may hold values from 0.5 to 1.5
- ln2_bias: float32 [2048], replicated, may hold values from -1 to 1
- w_up: bfloat16 [2048, 4096], P(None, 'mp'), may hold values from -0.125 to 0.125
- b_up: float32 [4096], P('mp'), may hold values from -1.5 to 1.5
- w_down: bfloat16 [4096, 2048], P('mp'), may hold values from -0.125 to 0.125
- b_down: float32 [2048], replicated, may hold values from -1 to 1
Outputs:
- out: bfloat16 [16384, 2048], P(('dp', 'mp'))
- grad_x: float32 [16384, 2048], P(('dp', 'mp'))
- grad_ln1_gain: float32 [2048], replicated
- grad_ln1_bias: float32 [2048], replicated
- grad_query: float32 [2048, 2048], P(None, 'mp')
- grad_key: float32 [2048, 2048], P(None, 'mp')
- grad_value: float32 [2048, 4096], P(None, 'mp')
- grad_gate: float32 [2048, 4096], P(None, 'mp')
- grad_out: float32 [4096, 2048], P('mp')
- grad_ln2_gain: float32 [2048], replicated
- grad_ln2_bias: float32 [2048], replicated
- grad_up: float32 [2048, 4096], P(None, 'mp')
- grad_b_up: float32 [4096], P('mp')
- grad_down: float32 [4096, 2048], P('mp')
- grad_b_down: float32 [2048], replicated
The draws below stay inside these ranges and needn't reach their ends.
Inputs may be any that keep to these rules, and one draw needn't show every extreme that they name: `lengths`: each row gives, in order, three documents that fill the group's 1024 tokens: the first and the last hold fewer than 128 tokens each (possibly none), so the middle one reaches from the group's first 128 tokens into its last 128; in at least one group the middle one fills all 1024 tokens.
All inputs are finite; a program needn't handle non-finite values.
Results may differ from the reference program's by a relative error of at most 0.03.
Values may be sent and summed in bfloat16 or wider, within the bound.
No kernel may reach another device: no remote copies, remote signals or barrier semaphores. Data moves between devices by JAX's collectives and lax.ppermute only.
A program may use at most 192 MiB of HBM per device.

```python
import math
import jax
import jax.numpy as jnp
from jax import lax

D = 2048
HEADS = 8
DK = 256
DV = 512
FF = 4096
GROUP = 1024
ROWS = 128
BLOCK = 512
QK = 2048
VW = 4096
TOKENS = 16384
N_DP = 16


def draw_lengths(key, part):
    key = jax.random.fold_in(key, 7)
    first_key, last_key, pick_key = jax.random.split(key, 3)
    first_len = jax.random.randint(first_key, (N_DP,), 0, ROWS, dtype=jnp.int32)
    last_len = jax.random.randint(last_key, (N_DP,), 0, ROWS, dtype=jnp.int32)
    chosen = jax.random.randint(pick_key, (), 0, N_DP, dtype=jnp.int32)
    whole_group = jnp.arange(N_DP, dtype=jnp.int32) == chosen
    first_len = jnp.where(whole_group, 0, first_len)
    last_len = jnp.where(whole_group, 0, last_len)
    middle_len = GROUP - first_len - last_len
    return jnp.stack([first_len, middle_len, last_len], -1).astype(jnp.int32)


def level_of(rng, shape, cuts, smallest, top_value):
    def one(axis_at, blocks):
        heights = jax.random.uniform(jax.random.fold_in(jax.random.fold_in(rng, 6), axis_at), (blocks,), jnp.float32, smallest / len(cuts), top_value / len(cuts))
        return jnp.repeat(jnp.exp(heights), shape[axis_at] // blocks).reshape((-1,) + (1,) * (len(shape) - axis_at - 1))

    level = one(*cuts[0])
    for cut in cuts[1:]:
        level = level * one(*cut)
    return level


def scatter_about(rng, dims, scale, bound, pieces=(), kind=jnp.bfloat16):
    loudness = level_of(rng, dims, pieces, -0.22, 0.18) if pieces else 1.0
    entries = jax.random.normal(rng, dims, jnp.float32) * scale * loudness
    return jnp.minimum(jnp.maximum(entries, -bound), bound).astype(kind)


def setup_inputs(seed: int = 0) -> dict:
    splits = jax.random.split(jax.random.key(seed), 17)
    return {
        "tokens_in": scatter_about(splits[0], (TOKENS, D), 1.0, 6.0, ((0, 128),)),
        "cotangent": scatter_about(splits[1], (TOKENS, D), 1.0, 6.0, ((0, 128),)),
        "lengths": draw_lengths(jax.random.fold_in(splits[16], 71), 0),
        "ln1_gain": jnp.clip(1.0 + 0.1 * jax.random.normal(splits[3], (D,), jnp.float32), 0.5, 1.5),
        "ln1_bias": scatter_about(splits[4], (D,), 0.2, 1.0, (), jnp.float32),
        "w_query": scatter_about(splits[5], (D, QK), D ** -0.5, 0.125, ((1, 8),)),
        "w_key": scatter_about(splits[6], (D, QK), D ** -0.5, 0.125, ((1, 8),)),
        "w_value": scatter_about(splits[7], (D, VW), D ** -0.5, 0.125, ((1, 8),)),
        "w_gate": scatter_about(splits[8], (D, VW), D ** -0.5, 0.125, ((1, 8),)),
        "w_out": scatter_about(splits[9], (VW, D), (VW // 2) ** -0.5, 0.125, ((0, 8),)),
        "ln2_gain": jnp.clip(1.0 + 0.1 * jax.random.normal(splits[10], (D,), jnp.float32), 0.5, 1.5),
        "ln2_bias": scatter_about(splits[11], (D,), 0.2, 1.0, (), jnp.float32),
        "w_up": scatter_about(splits[12], (D, FF), D ** -0.5, 0.125, ((1, 8),)),
        "b_up": scatter_about(splits[13], (FF,), 0.3, 1.5, ((0, 8),), jnp.float32),
        "w_down": scatter_about(splits[14], (FF, D), (FF // 2) ** -0.5, 0.125, ((0, 8),)),
        "b_down": scatter_about(splits[15], (D,), 0.2, 1.0, (), jnp.float32),
    }


norm_eps = 1e-05
group_eps = 1.0
highest = lax.Precision.HIGHEST

@jax.custom_vjp
def low(v):
    return lax.optimization_barrier(v.astype(jnp.bfloat16)).astype(jnp.float32)

@jax.custom_vjp
def low_back(v):
    return v

def low_keep(v):
    return (low(v), None)

def low_pass(kept, grad):
    return (grad,)

def back_keep(v):
    return (v, None)

def back_low(kept, grad):
    return (low(grad),)
low.defvjp(low_keep, low_pass)
low_back.defvjp(back_keep, back_low)

def layer_norm(inputs, gain_vec, bias_vec):
    centre = inputs - lax.optimization_barrier(jnp.mean(inputs, -1, keepdims=True))
    spread = lax.optimization_barrier(jnp.mean(centre * centre, -1, keepdims=True))
    return centre * lax.rsqrt(spread + norm_eps) * gain_vec + bias_vec

def rotate(inputs, cosine, sine_table):
    paired = inputs.reshape(inputs.shape[:-1] + (inputs.shape[-1] // 2, 2))
    turned = jnp.stack([-paired[..., 1], paired[..., 0]], -1).reshape(inputs.shape)
    return inputs * cosine + turned * sine_table

def layout(length_row, token_count):
    doc_ends = jnp.cumsum(length_row).astype(jnp.int32)
    doc_starts = (doc_ends - length_row).astype(jnp.int32)
    tokens = jnp.arange(token_count, dtype=jnp.int32)
    member = (tokens[:, None] >= doc_starts[None, :]) & (tokens[:, None] < doc_ends[None, :])
    numbers = jnp.arange(length_row.shape[0], dtype=jnp.int32)
    doc_ids = lax.optimization_barrier(jnp.sum(jnp.where(member, numbers[None, :], 0), -1)).astype(jnp.int32)
    offsets = lax.optimization_barrier(jnp.sum(jnp.where(member, doc_starts[None, :], 0), -1)).astype(jnp.int32)
    return (doc_ids, (tokens - offsets).astype(jnp.int32))

def angles(positions, head_width):
    half_width = head_width // 2
    ladder = jnp.arange(half_width, dtype=jnp.float32) / max(half_width - 1, 1)
    frequency = jnp.repeat(jnp.exp(-math.log(10000.0) * ladder), 2)
    phases = positions.astype(jnp.float32)[:, None] * frequency[None, :]
    return (jnp.cos(phases)[:, None, :], jnp.sin(phases)[:, None, :])

def decay_mask(row_docs, row_start, doc_ids, log_decay, block_len, group_tok):
    row_index = row_start + jnp.arange(block_len, dtype=jnp.int32)
    col_index = jnp.arange(group_tok, dtype=jnp.int32)
    distance = row_index[:, None] - col_index[None, :]
    visible = (distance >= 0) & (row_docs[:, None] == doc_ids[None, :])
    span_float = jnp.maximum(distance, 0).astype(log_decay.dtype)
    return jnp.where(visible[None], jnp.exp(span_float[None] * log_decay[:, None, None]), 0.0)

def gate_norm(retained, gate_pre):
    scale_inv = lax.rsqrt(lax.optimization_barrier(jnp.mean(retained * retained, -1, keepdims=True)) + group_eps)
    return jax.nn.silu(gate_pre) * (retained * scale_inv).reshape(gate_pre.shape)

def group_forward(inputs, doc_ids, positions, params):
    gain_one, bias_one, w_query, w_key, w_value, w_gate, w_out, gain_two, bias_two, w_up, b_up, w_down, b_down = params
    normed = low(layer_norm(inputs, gain_one, bias_one))
    queries = low_back(jnp.dot(normed, w_query, precision=highest)).reshape(GROUP, HEADS, DK)
    keys_all = low_back(jnp.dot(normed, w_key, precision=highest)).reshape(GROUP, HEADS, DK)
    values = low(low_back(jnp.dot(normed, w_value, precision=highest))).reshape(GROUP, HEADS, DV)
    gate_pre = low_back(jnp.dot(normed, w_gate, precision=highest))
    cosine, sine_table = angles(positions, DK)
    query_rot = low(rotate(queries, cosine, sine_table))
    key_rot = low(rotate(keys_all, cosine, sine_table))
    log_decay = jnp.log1p(-jnp.exp2(-5.0 - jnp.arange(HEADS, dtype=jnp.float32)))

    def retain(row_start):
        query_rows = lax.dynamic_slice_in_dim(query_rot, row_start, BLOCK, 0)
        row_docs = lax.dynamic_slice_in_dim(doc_ids, row_start, BLOCK, 0)
        weights_mask = decay_mask(row_docs, row_start, doc_ids, log_decay, BLOCK, GROUP)
        raw_scores = low_back(jnp.einsum('qhd,khd->hqk', query_rows, key_rot, precision=highest))
        scores = low(raw_scores * weights_mask)
        return low_back(jnp.einsum('hqk,khe->qhe', scores, values, precision=highest))
    row_starts = jnp.arange(GROUP // BLOCK, dtype=jnp.int32) * BLOCK
    retained = lax.map(jax.checkpoint(retain), row_starts).reshape(GROUP, HEADS, DV)
    gated = low(gate_norm(retained, gate_pre))
    middle = inputs + low_back(jnp.dot(gated, w_out, precision=highest))
    normed_two = low(layer_norm(middle, gain_two, bias_two))
    pre_act = low_back(jnp.dot(normed_two, w_up, precision=highest) + b_up)
    hidden = low(jax.nn.gelu(pre_act, approximate=False))
    return middle + low_back(jnp.dot(hidden, w_down, precision=highest)) + b_down

def reference(tokens_in, cotangent, lengths, ln1_gain, ln1_bias, w_query, w_key, w_value, w_gate, w_out, ln2_gain, ln2_bias, w_up, b_up, w_down, b_down):
    params = tuple((entry.astype(jnp.float32) for entry in (ln1_gain, ln1_bias, w_query, w_key, w_value, w_gate, w_out, ln2_gain, ln2_bias, w_up, b_up, w_down, b_down)))
    inputs = tokens_in.astype(jnp.float32).reshape(N_DP, GROUP, D)
    cot_groups = cotangent.astype(jnp.float32).reshape(N_DP, GROUP, D)
    doc_ids, positions = jax.vmap(lambda length_row: layout(length_row, GROUP))(lengths)

    def forward(stacked, weights_all):

        def scan_step(carried, members):
            return (carried, group_forward(members[0], members[1], members[2], weights_all))
        return lax.scan(scan_step, jnp.zeros((), jnp.float32), (stacked, doc_ids, positions))[1]
    result, pull_back = jax.vjp(forward, inputs, params)
    grad_inputs, weight_grads = pull_back(cot_groups)
    return (result.reshape(TOKENS, D).astype(jnp.bfloat16), grad_inputs.reshape(TOKENS, D), weight_grads[0], weight_grads[1], weight_grads[2], weight_grads[3], weight_grads[4], weight_grads[5], weight_grads[6], weight_grads[7], weight_grads[8], weight_grads[9], weight_grads[10], weight_grads[11], weight_grads[12])
```

```python
import functools
import math

import jax
import jax.numpy as jnp
import numpy as np
from jax import lax
from jax.experimental import pallas as pl
from jax.experimental.pallas import tpu as pltpu
from jax.sharding import Mesh
from jax.sharding import PartitionSpec as P

DK = 256
DV = 512
AXES = ("x", "yh", "c", "yl", "z")
DP = ("x", "yh", "c")
MP = ("yl", "z")
BF = jnp.bfloat16
F32 = jnp.float32
MIB = 1024 * 1024

norm_eps = 1e-05
group_eps = 1.0

WAVE_A = ((0, 0), (1, 0), (-1, 0), (0, 1))
WAVE_B = ((2, 0), (1, 1), (-1, 1), (2, 1))
ORDER = WAVE_A + WAVE_B


def after(value, *others):
    return lax.optimization_barrier((value, *others))[0]


class Line:
    def __init__(self):
        self.last = ()

    def hold(self, value):
        return after(value, *self.last) if self.last else value

    def done(self, value):
        self.last = (value,)
        return value

    def wait(self, *values):
        self.last = (*self.last, *values)


def plus(*terms):
    return functools.reduce(lambda u, v: u + v, [t.astype(F32) for t in terms])


def shifted(value, axis, step):
    size = lax.axis_size(axis)
    return lax.ppermute(value, axis, [((i + step) % size, i) for i in range(size)])


def by_sides(value, axis, way):
    size = lax.axis_size(axis)
    names = ("x", "c") if axis == "x" else ("c", axis)

    def flat(c, i):
        return i * 2 + c if axis == "x" else c * size + i

    pairs = []
    for c, step in ((0, way), (1, -way)):
        for i in range(size):
            pairs.append((flat(c, (i + step) % size), flat(c, i)))
    return lax.ppermute(value, names, pairs)


def across(value, axis):
    return by_sides(value, axis, 1)


def across_back(value, axis):
    return by_sides(value, axis, -1)


class Gather:
    def __init__(self, own):
        self.got = got = {(0, 0): own}
        got[1, 0] = shifted(own, "z", 1)
        got[-1, 0] = shifted(own, "z", -1)
        got[0, 1] = shifted(own, "yl", 1)

    def second(self, line):
        got = self.got
        line.wait(got[0, 1], got[1, 0], got[-1, 0])
        got[2, 0] = across(line.done(by_core(line.hold(got[1, 0]), got[-1, 0])), "z")
        got[1, 1] = shifted(got[0, 1], "z", 1)
        got[-1, 1] = shifted(got[0, 1], "z", -1)
        got[2, 1] = shifted(got[2, 0], "yl", 1)

    def wave(self, places):
        return [self.got[p] for p in places]


class LateGather(Gather):
    def __init__(self, own):
        self.got = {(0, 0): own, (0, 1): shifted(own, "yl", 1)}

    def sides(self, line):
        got = self.got
        own, other = line.hold(got[0, 0]), line.hold(got[0, 1])
        got[1, 0] = shifted(own, "z", 1)
        got[-1, 0] = shifted(own, "z", -1)
        got[1, 1] = shifted(other, "z", 1)
        got[-1, 1] = shifted(other, "z", -1)

    def second(self, line):
        got = self.got
        got[2, 0] = across(line.done(by_core(line.hold(got[1, 0]), got[-1, 0])), "z")

    def third(self, line):
        self.got[2, 1] = shifted(line.hold(self.got[2, 0]), "yl", 1)


class Scatter:
    def __init__(self, part):
        self.part = part
        self.far = shifted(part[2, 1], "yl", 1)
        self.up = shifted(part[1, 1], "z", -1)
        self.down = shifted(part[-1, 1], "z", 1)

    def relay(self, line):
        line.wait(self.far)
        self.passed = across_back(line.done(added(line.hold(self.part[2, 0]), self.far)), "z")

    def side(self, line):
        part = self.part
        line.wait(self.up, self.down)
        self.other = shifted(line.done(added(line.hold(part[0, 1]), self.up, self.down)), "yl", 1)

    def near(self, line):
        part = self.part
        line.wait(self.passed)
        up, down = pair(line.hold(part[1, 0]), part[-1, 0], self.passed)
        line.done(up)
        self.near_up = shifted(up, "z", -1)
        self.near_down = shifted(down, "z", 1)

    def terms(self):
        return [self.part[0, 0], self.other, self.near_up, self.near_down]


class Summed:
    def __init__(self, value, axes):
        self.value, self.left, self.come = value, [], None
        for axis in axes:
            size = lax.axis_size(axis)
            mates = ((1, 0),) if size == 2 else ((1, 0, 3, 2), (3, 2, 1, 0))
            self.left += [(axis, [(i, mate[i]) for i in range(size)]) for mate in mates]

    def step(self, line):
        if self.come is not None:
            line.wait(self.come)
            self.value = line.done(line.hold(self.value) + self.come)
            self.come = None
        if self.left:
            axis, pairs = self.left.pop(0)
            self.come = lax.ppermute(self.value, axis, pairs)


def dot_nn(a, b):
    return jnp.dot(a, b, preferred_element_type=F32)


def dot_nt(a, b):
    return lax.dot_general(a, b, (((1,), (1,)), ((), ())), preferred_element_type=F32)


def dot_tn(a, b):
    return lax.dot_general(a, b, (((0,), (0,)), ((), ())), preferred_element_type=F32)


def like(shape, dtype):
    return jax.ShapeDtypeStruct(shape, dtype)


def in_hbm(value):
    return pltpu.with_memory_space_constraint(value, pltpu.HBM)


NO_COST = pl.CostEstimate(flops=0, bytes_accessed=0, transcendentals=0)


def simple(body, outs, args, name, vmem, scalars=0, scratch=()):
    in_specs = [pl.BlockSpec(memory_space=pltpu.SMEM)] * scalars
    in_specs += [pl.BlockSpec(memory_space=pltpu.VMEM)] * (len(args) - scalars)
    return pl.pallas_call(
        body,
        in_specs=in_specs,
        out_specs=[pl.BlockSpec(memory_space=pltpu.VMEM)] * len(outs),
        out_shape=outs,
        scratch_shapes=list(scratch),
        compiler_params=pltpu.CompilerParams(vmem_limit_bytes=vmem * MIB),
        cost_estimate=NO_COST,
        name=name,
    )(*args)


def centred(values):
    centre = values - jnp.mean(values, -1, keepdims=True)
    scale = lax.rsqrt(jnp.mean(centre * centre, -1, keepdims=True) + norm_eps)
    return centre * scale, scale


def norm_kernel(inputs, gain, bias, out):
    xhat, _ = centred(inputs[...].astype(F32))
    out[...] = (xhat * gain[...] + bias[...]).astype(BF)


def norm(inputs, gain, bias):
    return simple(norm_kernel, [like(inputs.shape, BF)], [inputs, gain, bias], "norm", 6)[0]


def middle_kernel(inputs, own, side, up, down, gain, bias, middle, out):
    value = inputs[...].astype(F32) + plus(own[...], side[...], up[...], down[...])
    middle[...] = value
    xhat, _ = centred(value)
    out[...] = (xhat * gain[...] + bias[...]).astype(BF)


def middle_norm(inputs, terms, gain, bias):
    outs = [like(inputs.shape, F32), like(inputs.shape, BF)]
    return simple(middle_kernel, outs, [inputs, *terms, gain, bias], "middle", 10)


def norm_back(xhat, scale, grad, gain):
    e = grad * gain
    return scale * (e - jnp.mean(e, -1, keepdims=True) - xhat * jnp.mean(e * xhat, -1, keepdims=True))


def middle_back_kernel(middle, cot, own, side, up, down, gain, grad, low, sums):
    xhat, scale = centred(middle[...])
    term = plus(own[...], side[...], up[...], down[...])
    dy = cot[...].astype(F32)
    value = dy + norm_back(xhat, scale, term, gain[...])
    grad[...] = value
    low[...] = value.astype(BF)
    sums[0:1, :] = jnp.sum(term * xhat, 0, keepdims=True)
    sums[1:2, :] = jnp.sum(term, 0, keepdims=True)
    sums[2:3, :] = jnp.sum(dy, 0, keepdims=True)


def middle_back(middle, cot, terms, gain):
    outs = [like(middle.shape, F32), like(middle.shape, BF), like((3, middle.shape[1]), F32)]
    return simple(middle_back_kernel, outs, [middle, cot, *terms, gain], "middle_back", 12)


def input_back_kernel(inputs, middle_grad, own, side, up, down, gain, grad, sums):
    xhat, scale = centred(inputs[...].astype(F32))
    term = plus(own[...], side[...], up[...], down[...])
    grad[...] = middle_grad[...] + norm_back(xhat, scale, term, gain[...])
    sums[0:1, :] = jnp.sum(term * xhat, 0, keepdims=True)
    sums[1:2, :] = jnp.sum(term, 0, keepdims=True)


def input_back(inputs, middle_grad, terms, gain):
    outs = [like(inputs.shape, F32), like((2, inputs.shape[1]), F32)]
    return simple(input_back_kernel, outs, [inputs, middle_grad, *terms, gain], "input_back", 12)


def angle_tables(rows, blocks):
    half = DK // 2
    frequency = np.repeat(np.exp(-math.log(10000.0) * np.arange(half) / max(half - 1, 1)), 2)
    inner = np.arange(rows)[:, None] * frequency[None, :]
    outer = (np.arange(blocks) * rows)[:, None] * frequency[None, :]
    return [jnp.asarray(t, F32) for t in (np.cos(inner), np.sin(inner), np.cos(outer), np.sin(outer))]


def turn(values, cosine, sine, back):
    lane = lax.broadcasted_iota(jnp.int32, values.shape, 1)
    even = lane % 2 == 0
    if back:
        turned = values * sine
        return values * cosine + jnp.where(even, pltpu.roll(turned, DK - 1, 1), -pltpu.roll(turned, 1, 1))
    return values * cosine + jnp.where(even, -pltpu.roll(values, DK - 1, 1), pltpu.roll(values, 1, 1)) * sine


def block_angles(marks, number, tables):
    cos_in, sin_in, cos_out, sin_out = tables
    rows = cos_in.shape[0]
    block, first, second = marks[number], marks[8], marks[9]

    def joined(outer, inner):
        co, so = cos_out[pl.ds(outer, 1), :], sin_out[pl.ds(outer, 1), :]
        ci, si = cos_in[inner, :], sin_in[inner, :]
        return ci * co - si * so, si * co + ci * so

    cosine, sine = joined(block, slice(0, rows))
    cos_one, sin_one = joined(0, pl.ds(lax.rem(first, rows), 1))
    last = jnp.minimum(lax.div(second, rows), cos_out.shape[0] - 1)
    cos_two, sin_two = joined(last, pl.ds(lax.rem(second, rows), 1))
    token = block * rows + lax.broadcasted_iota(jnp.int32, (rows, 1), 0)
    back_cos = jnp.where(token >= second, cos_two, jnp.where(token >= first, cos_one, 1.0))
    back_sin = jnp.where(token >= second, sin_two, jnp.where(token >= first, sin_one, 0.0))
    return cosine * back_cos + sine * back_sin, sine * back_cos - cosine * back_sin


def pack(blocks, out):
    rows = blocks[0].shape[0]
    for n, block in enumerate(blocks):
        out[n * rows : (n + 1) * rows, :] = block[...]


def unpack(value, first, outs):
    rows = outs[0].shape[0]
    for n in range(value.shape[0] // rows):
        out = outs[first + n]
        out[...] = value[n * rows : (n + 1) * rows, :].astype(out.dtype)


def heads_kernel(marks, b0, b1, b2, b3, wq, wk, wv, wg, ci, si, co, so, x, qr, kr, vb, gate, *, first):
    pack((b0, b1, b2, b3), x)
    rows = b0.shape[0]
    q = dot_nn(x[...], wq[...])
    k = dot_nn(x[...], wk[...])
    for n in range(4):
        cosine, sine = block_angles(marks, first + n, (ci, si, co, so))
        at = slice(n * rows, (n + 1) * rows)
        qr[at, :] = turn(q[at, :], cosine, sine, False).astype(BF)
        kr[at, :] = turn(k[at, :], cosine, sine, False).astype(BF)
    vb[...] = dot_nn(x[...], wv[...]).astype(BF)
    gate[...] = dot_nn(x[...], wg[...])


def heads(marks, blocks, weights, tables, first):
    rows, width = blocks[0].shape
    n = 4 * rows
    outs = [like((n, width), BF), like((n, DK), BF), like((n, DK), BF), like((n, DV), BF), like((n, DV), F32)]
    return simple(
        functools.partial(heads_kernel, first=first), outs, [marks, *blocks, *weights, *tables], "heads", 20, 1
    )


def places_of(marks, first, rows, axis):
    shape = (rows, 1) if axis == 0 else (1, rows)
    lane = lax.broadcasted_iota(jnp.int32, shape, axis)
    return jnp.concatenate([marks[first + n] * rows + lane for n in range(4)], axis)


def row_marks(marks, decay, first, rows):
    place = places_of(marks, first, rows, 0)
    low = jnp.where(place >= marks[9], marks[9], jnp.where(place >= marks[8], marks[8], 0))
    return place, low, jnp.exp(place.astype(F32) * decay[0])


def col_marks(marks, decay, first, rows):
    place = places_of(marks, first, rows, 1)
    return place, jnp.exp(place.astype(F32) * -decay[0])


def mask_of(at, row, col):
    place, low, fade = (m[at, :] for m in row)
    seen = (col[0] <= place) & (col[0] >= low)
    return jnp.where(seen, fade * col[1], 0.0)


def retain_kernel(
    marks, decay, qr, kr_a, kr_b, vb_a, vb_b, gate, w_out, ret, gated, *outs, first
):
    half = kr_a.shape[0]
    tile = qr.shape[0] // 2
    rows = half // 4
    row = row_marks(marks, decay, first, rows)
    cols = [col_marks(marks, decay, n, rows) for n in (0, 4)]
    for i in range(2):
        at = slice(i * tile, (i + 1) * tile)
        out = None
        for k, v, col in ((kr_a, vb_a, cols[0]), (kr_b, vb_b, cols[1])):
            scores = (dot_nt(qr[at, :], k[...]) * mask_of(at, row, col)).astype(BF)
            term = dot_nn(scores, v[...])
            out = term if out is None else out + term
        ret[at, :] = out
        scale = lax.rsqrt(jnp.mean(out * out, -1, keepdims=True) + group_eps)
        g = gate[at, :]
        low = (g / (1.0 + jnp.exp(-g)) * out * scale).astype(BF)
        gated[at, :] = low
        unpack(dot_nn(low, w_out[...]), i * 2, outs)


def block_outs(places, shape):
    return [like(shape, F32 if p == (0, 0) else BF) for p in places]


def retain(marks, decay, places, q, ks, vs, gate, w_out):
    rows = q.shape[0]
    outs = [like((rows, DV), F32), like((rows, DV), BF)] + block_outs(places, (rows // 4, w_out.shape[1]))
    body = functools.partial(retain_kernel, first=ORDER.index(places[0]))
    got = simple(body, outs, [marks, decay, q, *ks, *vs, gate, w_out], "retain", 16, 2)
    return got[0], got[1], dict(zip(places, got[2:]))


def hidden_grad_kernel(b0, b1, b2, b3, w_down, packed, out):
    pack((b0, b1, b2, b3), packed)
    out[...] = dot_nt(packed[...], w_down[...])


def hidden_grad(blocks, w_down):
    rows, width = blocks[0].shape
    outs = [like((4 * rows, width), BF), like((4 * rows, w_down.shape[0]), F32)]
    return simple(hidden_grad_kernel, outs, [*blocks, w_down], "hidden_grad", 12)


def feed_kernel(b0, b1, b2, b3, w_up, b_up, dh, packed, hidden, dpre, bias_sum, *outs):
    pack((b0, b1, b2, b3), packed)
    tile = packed.shape[0] // 2
    total = None
    for i in range(2):
        at = slice(i * tile, (i + 1) * tile)
        pre = dot_nn(packed[at, :], w_up[...]) + b_up[...]
        below = 0.5 * (1.0 + lax.erf(pre * (1.0 / math.sqrt(2.0))))
        hidden[at, :] = (pre * below).astype(BF)
        slope = below + pre * jnp.exp(-0.5 * pre * pre) * (1.0 / math.sqrt(2.0 * math.pi))
        low = (dh[at, :] * slope).astype(BF)
        dpre[at, :] = low
        column = jnp.sum(low.astype(F32), 0, keepdims=True)
        total = column if total is None else total + column
        unpack(dot_nt(low, w_up[...]), i * 2, outs)
    bias_sum[...] = total


def feed(places, blocks, w_up, b_up, dh):
    rows, width = blocks[0].shape
    hidden = w_up.shape[1]
    n = 4 * rows
    outs = [like((n, width), BF), like((n, hidden), BF), like((n, hidden), BF), like((1, hidden), F32)]
    outs += block_outs(places, (rows, width))
    got = simple(feed_kernel, outs, [*blocks, w_up, b_up, dh], "feed", 16)
    return *got[:4], dict(zip(places, got[4:]))


def feed_out_kernel(hidden, w_down, *outs):
    tile = hidden.shape[0] // 2
    for i in range(2):
        unpack(dot_nn(hidden[i * tile : (i + 1) * tile, :], w_down[...]), i * 2, outs)


def feed_out(places, hidden, w_down):
    outs = block_outs(places, (hidden.shape[0] // 4, w_down.shape[1]))
    return dict(zip(places, simple(feed_out_kernel, outs, [hidden, w_down], "feed_out", 10)))


def gate_back_kernel(b0, b1, b2, b3, w_out, ret, gate, packed, dret, dgate):
    pack((b0, b1, b2, b3), packed)
    tile = packed.shape[0] // 2
    for i in range(2):
        at = slice(i * tile, (i + 1) * tile)
        dgt = dot_nt(packed[at, :], w_out[...])
        g = gate[at, :]
        out = ret[at, :]
        sig = 1.0 / (1.0 + jnp.exp(-g))
        scale = lax.rsqrt(jnp.mean(out * out, -1, keepdims=True) + group_eps)
        y = out * scale
        dgate[at, :] = (dgt * y * (sig * (1.0 + g * (1.0 - sig)))).astype(BF)
        e = dgt * (g * sig)
        dret[at, :] = (scale * (e - y * jnp.mean(e * y, -1, keepdims=True))).astype(BF)


def gate_back(blocks, w_out, ret, gate):
    rows, width = blocks[0].shape
    outs = [like((4 * rows, width), BF), like((4 * rows, DV), BF), like((4 * rows, DV), BF)]
    return simple(gate_back_kernel, outs, [*blocks, w_out, ret, gate], "gate_back", 16)


def retain_back_kernel(
    marks, decay, qr_a, qr_b, kr_a, kr_b, vb_a, vb_b, dret_a, dret_b, ci, si, co, so,
    grads_a, grads_b, dk_sum, dv_sum,
):
    half = qr_a.shape[0]
    tile = half // 2
    rows = ci.shape[0]
    tables = (ci, si, co, so)

    def turned(value, block):
        cosine, sine = block_angles(marks, block, tables)
        return turn(value, cosine, sine, True).astype(BF)

    row_parts = [row_marks(marks, decay, n, rows) for n in (0, 4)]
    col_parts = [col_marks(marks, decay, n, rows) for n in (0, 4)]
    for i in range(4):
        q_ref, dret_ref, grads = (qr_a, dret_a, grads_a) if i < 2 else (qr_b, dret_b, grads_b)
        at = slice(i % 2 * tile, (i % 2 + 1) * tile)
        q = q_ref[at, :]
        dret = dret_ref[at, :]
        dq = None
        for j, (k, v) in enumerate(((kr_a, vb_a), (kr_b, vb_b))):
            cols = slice(j * half, (j + 1) * half)
            mask = mask_of(at, row_parts[i // 2], col_parts[j])
            scores = (dot_nt(q, k[...]) * mask).astype(BF)
            raw = (dot_nt(dret, v[...]) * mask).astype(BF)
            term = dot_nn(raw, k[...])
            dq = term if dq is None else dq + term
            if i == 0:
                dk_sum[cols, :] = dot_tn(raw, q)
                dv_sum[cols, :] = dot_tn(scores, dret)
            else:
                dk_sum[cols, :] += dot_tn(raw, q)
                dv_sum[cols, :] += dot_tn(scores, dret)
        for n in range(tile // rows):
            grads[i % 2 * tile + n * rows : i % 2 * tile + (n + 1) * rows, 0:DK] = turned(
                dq[n * rows : (n + 1) * rows, :], i * (tile // rows) + n
            )
    for j, grads in enumerate((grads_a, grads_b)):
        for n in range(half // rows):
            at = slice(j * half + n * rows, j * half + (n + 1) * rows)
            grads[n * rows : (n + 1) * rows, DK : 2 * DK] = turned(dk_sum[at, :], j * (half // rows) + n)
        grads[:, 2 * DK : 2 * DK + DV] = dv_sum[j * half : (j + 1) * half, :].astype(BF)


def retain_back(marks, decay, qs, ks, vs, drets, tables):
    half = qs[0].shape[0]
    outs = [like((half, 2 * DK + DV), BF)] * 2
    scratch = [pltpu.VMEM((2 * half, DK), F32), pltpu.VMEM((2 * half, DV), F32)]
    args = [marks, decay, *qs, *ks, *vs, *drets, *tables]
    return simple(retain_back_kernel, outs, args, "retain_back", 18, 2, scratch)


def heads_back_kernel(dqkv, dgate, wq, wk, wv, wg, *outs):
    tile = dqkv.shape[0] // 2
    for i in range(2):
        at = slice(i * tile, (i + 1) * tile)
        total = dot_nt(dqkv[at, 0:DK], wq[...]) + dot_nt(dqkv[at, DK : 2 * DK], wk[...])
        total = total + dot_nt(dqkv[at, 2 * DK : 2 * DK + DV], wv[...]) + dot_nt(dgate[at, :], wg[...])
        unpack(total, i * 2, outs)


def heads_back(places, dqkv, dgate, weights):
    outs = block_outs(places, (dqkv.shape[0] // 4, weights[0].shape[0]))
    return dict(zip(places, simple(heads_back_kernel, outs, [dqkv, dgate, *weights], "heads_back", 18)))


def added_kernel(*refs):
    refs[-1][...] = plus(*[r[...] for r in refs[:-1]]).astype(BF)


def added(*terms):
    return simple(added_kernel, [like(terms[0].shape, BF)], list(terms), "added", 6)[0]


def chosen_kernel(core, first, second, out):
    @pl.when(core[0] == 0)
    def _():
        out[...] = first[...]

    @pl.when(core[0] != 0)
    def _():
        out[...] = second[...]


def by_core(first, second):
    core = lax.axis_index("c").astype(jnp.int32)[None]
    return simple(chosen_kernel, [like(first.shape, first.dtype)], [core, first, second], "chosen", 6, 1)[0]


def pair_kernel(core, up, down, passed, new_up, new_down):
    first = core[0] == 0
    value = passed[...].astype(F32)
    new_up[...] = (up[...].astype(F32) + jnp.where(first, value, 0.0)).astype(BF)
    new_down[...] = (down[...].astype(F32) + jnp.where(first, 0.0, value)).astype(BF)


def pair(up, down, passed):
    core = lax.axis_index("c").astype(jnp.int32)[None]
    return simple(pair_kernel, [like(up.shape, BF)] * 2, [core, up, down, passed], "pair", 6, 1)


def near_kernel(near, passed, out):
    rows = passed.shape[0]
    out[0:rows, :] = plus(near[0:rows, :], passed[...]).astype(BF)
    out[rows : 2 * rows, :] = near[rows : 2 * rows, :]


def quarter_kernel(own, come, swapped, out):
    rows = own.shape[0]
    out[...] = plus(own[...], come[0:rows, :], swapped[rows : 2 * rows, :]).astype(BF)


def both_kernel(first, second, out):
    rows = first.shape[0]
    out[0:rows, :] = first[...]
    out[rows : 2 * rows, :] = second[...]


def upper_kernel(both, out):
    out[...] = both[0 : out.shape[0], :]


def weight_kernel(places, *refs, counts, rest):
    refs = list(refs)
    lefts, rights = [], []
    for count in counts:
        lefts.append([refs.pop(0) for _ in range(count)])
        rights.append([refs.pop(0) for _ in range(count)])
    more = refs.pop(0) if rest else None
    step = pl.program_id(0)
    at = 0
    parts = []
    for left, right in zip(lefts, rights):
        total = functools.reduce(lambda u, v: u + v, [dot_tn(l[...], r[...]) for l, r in zip(left, right)])
        width = total.shape[1]
        if rest:
            total = total + more[:, at : at + width].astype(F32)
        parts.append((at, width, total.astype(BF)))
        at += width
    if not rest:
        for at, width, total in parts:
            refs[0][:, at : at + width] = total
        return
    two, near, own = refs
    rows = two.shape[0]
    for k, (out, first) in enumerate(((two, 0), (near, 0), (near, rows), (own, 0))):

        @pl.when(step == k)
        def _(out=out, first=first):
            for at, width, total in parts:
                out[first : first + rows, at : at + width] = total


def weight_parts(pairs, places, first, more):
    piece = pairs[0][0][0].shape[1] // 8
    specs, args, columns = [], [], 0
    for lefts, rights in pairs:
        for left in lefts:
            specs.append(pl.BlockSpec((left.shape[0], piece), lambda i, places: (0, places[first + i])))
            args.append(left)
        for right, shape, at in rights:
            specs.append(pl.BlockSpec(shape, lambda i, places, at=at: at))
            args.append(right)
        columns += rights[0][1][1]
    if more is None:
        out_specs = pl.BlockSpec((piece, columns), lambda i, places: (i, 0))
        out_shape = like((4 * piece, columns), BF)
    else:
        specs.append(pl.BlockSpec((piece, columns), lambda i, places: (i, 0)))
        args.append(more)
        out_shape = [like((piece * n, columns), BF) for n in (1, 2, 1)]
        out_specs = [pl.BlockSpec(o.shape, lambda i, places: (0, 0)) for o in out_shape]
    return pl.pallas_call(
        functools.partial(weight_kernel, counts=[len(lefts) for lefts, _ in pairs], rest=more is not None),
        grid_spec=pltpu.PrefetchScalarGridSpec(num_scalar_prefetch=1, grid=(4,), in_specs=specs, out_specs=out_specs),
        out_shape=out_shape,
        compiler_params=pltpu.CompilerParams(vmem_limit_bytes=16 * MIB),
        cost_estimate=NO_COST,
        name="weight_parts",
    )(places, *args)


def piece_places():
    size = lax.axis_size("x")
    xi = lax.axis_index("x")

    def number(half, step):
        return half * size + (xi + step + size) % size

    def kept(core):
        way = 1 - 2 * core
        return [number(core, 2), number(core, way), number(1 - core, way), number(core, 0)]

    core = lax.axis_index("c")
    way = 1 - 2 * core
    last = [number(core, 0), number(1 - core, 0), number(core, -way), number(1 - core, -way)]
    last += [number(1 - core, way), number(core, way), number(core, 2), number(1 - core, 2)]
    return [jnp.stack(p).astype(jnp.int32) for p in (kept(1 - core) + kept(core), last)]


def holding(line, pairs):
    (lefts, rights), *more = pairs
    return [([line.hold(lefts[0]), *lefts[1:]], rights), *more]


class OverGroups:
    def __init__(self, places):
        self.places = places

    def send(self, line, pairs):
        self.pairs = pairs
        self.other = shifted(line.done(weight_parts(holding(line, pairs), self.places, 0, None)), "c", 1)

    def keep(self, line):
        line.wait(self.other)
        two, self.side, self.own = weight_parts(holding(line, self.pairs), self.places, 4, self.other)
        line.done(self.own)
        self.passed = across_back(two, "x")

    def near(self, line):
        line.wait(self.passed)
        shape = self.side.shape
        side = simple(near_kernel, [like(shape, BF)], [line.hold(self.side), self.passed], "near", 8)[0]
        self.come = across_back(line.done(side), "x")

    def half(self, line):
        line.wait(self.come)
        self.come = line.done(line.hold(self.come))
        self.swapped = shifted(self.come, "c", 1)

    def quarter(self, line):
        line.wait(self.swapped)
        args = [line.hold(self.own), self.come, self.swapped]
        self.mine = line.done(simple(quarter_kernel, [like(self.own.shape, BF)], args, "quarter", 8)[0])
        self.theirs = shifted(self.mine, "yh", 1)

    def whole(self, line):
        line.wait(self.theirs)
        self.mine = line.done(added(line.hold(self.mine), self.theirs))
        self.swapped = shifted(self.mine, "c", 1)

    def spread(self, line):
        line.wait(self.swapped)
        rows, width = self.mine.shape
        args = [line.hold(self.mine), self.swapped]
        self.both = line.done(simple(both_kernel, [like((2 * rows, width), BF)], args, "both", 8)[0])
        self.come = across_back(self.both, "x")

    def last(self, line):
        line.wait(self.come)
        upper = simple(upper_kernel, [like(self.mine.shape, BF)], [line.hold(self.come)], "upper", 6)[0]
        self.two = across_back(line.done(upper), "x")

    def swap(self, line):
        line.wait(self.two)
        come, two = line.hold(self.come), line.hold(self.two)
        self.moved = [shifted(come, "c", 1), shifted(two, "c", 1)]

    def pieces(self, line):
        line.wait(*self.moved)
        return [line.hold(self.both), self.come, self.moved[0], self.two, self.moved[1]]


def place_kernel(places, *refs, columns, turned, counts):
    step = pl.program_id(0)
    pieces, outs = refs[: len(counts)], refs[len(counts) :]
    first = 0
    for piece, count in zip(pieces, counts):

        @pl.when((step >= first) & (step < first + count))
        def _(piece=piece):
            at = 0
            for out, width, turn_it in zip(outs, columns, turned):
                value = piece[:, at : at + width].astype(F32)
                out[...] = value.T if turn_it else value
                at += width

        first += count


def placed(pieces, places, columns, turned):
    rows = min(p.shape[0] for p in pieces)
    counts = [p.shape[0] // rows for p in pieces]
    out_specs, out_shape, in_specs = [], [], []
    for width, turn_it in zip(columns, turned):
        if turn_it:
            out_specs.append(pl.BlockSpec((width, rows), lambda i, places: (0, places[i])))
            out_shape.append(jax.ShapeDtypeStruct((width, 8 * rows), F32))
        else:
            out_specs.append(pl.BlockSpec((rows, width), lambda i, places: (places[i], 0)))
            out_shape.append(jax.ShapeDtypeStruct((8 * rows, width), F32))
    first = 0
    for piece, count in zip(pieces, counts):
        in_specs.append(
            pl.BlockSpec((rows, piece.shape[1]), lambda i, places, f=first, n=count: (jnp.clip(i - f, 0, n - 1), 0))
        )
        first += count
    return pl.pallas_call(
        functools.partial(place_kernel, columns=columns, turned=turned, counts=counts),
        grid_spec=pltpu.PrefetchScalarGridSpec(
            num_scalar_prefetch=1, grid=(8,), in_specs=in_specs, out_specs=out_specs
        ),
        out_shape=out_shape,
        compiler_params=pltpu.CompilerParams(vmem_limit_bytes=16 * MIB),
        cost_estimate=NO_COST,
        name="placed",
    )(places, *pieces)


def local(
    tokens_in,
    cotangent,
    lengths,
    ln1_gain,
    ln1_bias,
    w_query,
    w_key,
    w_value,
    w_gate,
    w_out,
    ln2_gain,
    ln2_bias,
    w_up,
    b_up,
    w_down,
    b_down,
):
    rows = tokens_in.shape[0]
    half = rows * 4
    z_size = lax.axis_size("z")
    blocks = z_size * lax.axis_size("yl")
    zi = lax.axis_index("z")
    yi = lax.axis_index("yl")
    ends = jnp.cumsum(lengths[0])
    marks = [((yi + dy) % 2) * z_size + (zi + dz) % z_size for dz, dy in ORDER] + [ends[0], ends[1]]
    marks = jnp.stack([m.astype(jnp.int32) for m in marks])
    decay = jnp.log1p(-jnp.exp2(-5.0 - lax.axis_index(MP).astype(F32)))[None]
    tables = angle_tables(rows, blocks)
    places, final = piece_places()
    weights = (w_query, w_key, w_value, w_gate)
    heads_weights = tuple(in_hbm(w) for w in weights)
    gain_one, bias_one, gain_two, bias_two = (v[None, :] for v in (ln1_gain, ln1_bias, ln2_gain, ln2_bias))
    square = (half, DV)
    line = Line()

    xg = Gather(line.done(norm(tokens_in, gain_one, bias_one)))
    cg = LateGather(line.hold(cotangent))
    line.done(marks)
    xg.second(line)
    got = xg.got
    line.wait(got[2, 0], cg.got[0, 1])
    cg.sides(line)
    x_a, q_a, k_a, v_a, gate_a = heads(
        marks, [line.hold(got[0, 0]), got[1, 0], got[-1, 0], got[0, 1]], heads_weights, tables, 0
    )
    line.done(q_a)
    line.wait(got[1, 1], got[-1, 1], got[2, 1])
    x_b, q_b, k_b, v_b, gate_b = heads(
        marks, [line.hold(got[2, 0])] + xg.wave(WAVE_B[1:]), heads_weights, tables, 4
    )
    line.done(q_b)
    ks, vs = (k_a, k_b), (v_a, v_b)
    ret_b, gated_b, part_b = retain(marks, decay, WAVE_B, q_b, ks, vs, gate_b, w_out)
    line.done(gated_b)
    cot = cg.got
    line.wait(cot[1, 0], cot[-1, 0], cot[1, 1], cot[-1, 1])
    ret_a, gated_a, part_a = retain(marks, decay, WAVE_A, line.hold(q_a), ks, vs, gate_a, w_out)
    line.done(gated_a)
    rs = Scatter({**part_a, **part_b})
    rs.relay(line)
    rs.side(line)
    cg.second(line)
    rs.near(line)
    cot_a, dh_a = hidden_grad([line.hold(cot[0, 0])] + cg.wave(WAVE_A[1:]), w_down)
    line.done(dh_a)
    line.wait(cot[2, 0])
    cg.third(line)
    first, *others = rs.terms()
    line.wait(*others)
    middle, normed_two = middle_norm(tokens_in, [line.hold(first), *others], gain_two, bias_two)

    ng = Gather(line.done(normed_two))
    line.wait(cot[2, 1])
    cot_b, dh_b = hidden_grad([line.hold(cot[2, 0])] + cg.wave(WAVE_B[1:]), w_down)
    line.done(dh_b)
    ng.second(line)
    got = ng.got
    line.wait(got[2, 0])
    n_a, hid_a, dpre_a, bsum_a, part_a = feed(
        WAVE_A, [line.hold(got[0, 0]), got[1, 0], got[-1, 0], got[0, 1]], w_up, b_up[None, :], dh_a
    )
    line.done(bsum_a)
    line.wait(got[1, 1], got[-1, 1], got[2, 1])
    n_b, hid_b, dpre_b, bsum_b, part_b = feed(
        WAVE_B, [line.hold(got[2, 0])] + ng.wave(WAVE_B[1:]), w_up, b_up[None, :], dh_b
    )
    line.done(bsum_b)
    rs = Scatter({**part_a, **part_b})
    out_b = feed_out(WAVE_B, line.hold(hid_b), w_down)
    line.done(out_b[2, 1])
    out_a = feed_out(WAVE_A, line.hold(hid_a), w_down)
    line.done(out_a[0, 1])
    rs.relay(line)
    rs.side(line)
    feed_sums = OverGroups(places)
    feed_sums.send(
        line,
        [
            ([n_a, n_b], [(dpre_a, dpre_a.shape, (0, 0)), (dpre_b, dpre_b.shape, (0, 0))]),
            ([cot_a, cot_b], [(hid_a, hid_a.shape, (0, 0)), (hid_b, hid_b.shape, (0, 0))]),
        ],
    )
    rs.near(line)
    feed_sums.keep(line)
    first, *others = rs.terms()
    line.wait(*others)
    grad_middle, branch, early = middle_back(middle, cotangent, [line.hold(first), *others], gain_two)

    bg = Gather(line.done(branch))
    feed_sums.near(line)
    bg.second(line)
    got = bg.got
    line.wait(got[2, 0])
    br_a, dret_a, dgate_a = gate_back(
        [line.hold(got[0, 0]), got[1, 0], got[-1, 0], got[0, 1]], w_out, ret_a, gate_a
    )
    line.done(dret_a)
    feed_sums.half(line)
    feed_sums.quarter(line)
    line.wait(got[1, 1], got[-1, 1], got[2, 1])
    br_b, dret_b, dgate_b = gate_back([line.hold(got[2, 0])] + bg.wave(WAVE_B[1:]), w_out, ret_b, gate_b)
    line.done(dret_b)
    gate_sums = OverGroups(places)
    gate_sums.send(
        line,
        [
            ([x_a, x_b], [(dgate_a, square, (0, 0)), (dgate_b, square, (0, 0))]),
            ([br_a, br_b], [(gated_a, square, (0, 0)), (gated_b, square, (0, 0))]),
        ],
    )
    dqkv_a, dqkv_b = retain_back(marks, decay, (q_a, q_b), ks, vs, (line.hold(dret_a), dret_b), tables)
    line.done(dqkv_b)
    gate_sums.keep(line)
    feed_sums.whole(line)
    part_b = heads_back(WAVE_B, line.hold(dqkv_b), dgate_b, weights)
    line.done(part_b[2, 1])
    part_a = heads_back(WAVE_A, line.hold(dqkv_a), dgate_a, weights)
    line.done(part_a[0, 1])
    rs = Scatter({**part_a, **part_b})
    gate_sums.near(line)
    head_sums = OverGroups(places)
    head_sums.send(line, [([x_a, x_b], [(dqkv_a, dqkv_a.shape, (0, 0)), (dqkv_b, dqkv_b.shape, (0, 0))])])
    rs.relay(line)
    rs.side(line)
    head_sums.keep(line)
    gate_sums.half(line)
    gate_sums.quarter(line)
    rs.near(line)
    head_sums.near(line)
    line.wait(rs.other)
    feed_sums.spread(line)
    first, *others = rs.terms()
    line.wait(*others)
    grad_x, late = input_back(tokens_in, grad_middle, [line.hold(first), *others], gain_one)
    line.done(late)
    sums = Summed(line.done(jnp.concatenate([late, early], 0)), ("z", "yl"))
    gate_sums.whole(line)
    gate_sums.spread(line)
    sums.step(line)
    head_sums.half(line)
    head_sums.quarter(line)
    sums.step(line)
    sums.step(line)
    out_rs = Scatter({**out_a, **{p: line.hold(v) for p, v in out_b.items()}})
    feed_sums.last(line)
    gate_sums.last(line)
    head_sums.whole(line)
    head_sums.spread(line)
    sums.step(line)
    wide = jnp.pad(bsum_a + bsum_b, ((0, 0), (0, early.shape[1] - bsum_a.shape[1])))
    sums = Summed(line.done(jnp.concatenate([line.hold(sums.value), wide], 0)), ("c", "yh", "x"))
    sums.step(line)
    out_rs.relay(line)
    out_rs.side(line)
    sums.step(line)
    feed_sums.swap(line)
    grad_up, grad_down = placed(feed_sums.pieces(line), final, (w_up.shape[1], w_down.shape[0]), (False, True))
    line.done(grad_up)
    gate_sums.swap(line)
    grad_gate, grad_out = placed(gate_sums.pieces(line), final, (DV, DV), (False, True))
    line.done(grad_gate)
    sums.step(line)
    head_sums.last(line)
    out_rs.near(line)
    sums.step(line)
    head_sums.swap(line)
    sums.step(line)
    grad_query, grad_key, grad_value = placed(head_sums.pieces(line), final, (DK, DK, DV), (False, False, False))
    line.done(grad_query)
    sums = sums.value
    b_up_sum = sums[5, : bsum_a.shape[1]]
    result = middle + plus(*out_rs.terms()) + b_down
    return (
        result.astype(BF),
        grad_x,
        sums[0],
        sums[1],
        grad_query,
        grad_key,
        grad_value,
        grad_gate,
        grad_out,
        sums[2],
        sums[3],
        grad_up,
        b_up_sum,
        grad_down,
        sums[4],
    )


def solution(mesh):
    split = Mesh(mesh.devices.reshape(4, 2, 2, 2, 4), AXES)
    rows = P(AXES, None)
    cols = P(None, MP)
    mp_rows = P(MP, None)
    return jax.shard_map(
        local,
        mesh=split,
        in_specs=(
            rows, rows, P(DP, None), P(), P(), cols, cols, cols, cols, mp_rows, P(), P(), cols, P(MP), mp_rows, P(),
        ),
        out_specs=(
            rows, rows, P(), P(), cols, cols, cols, cols, mp_rows, P(), P(), cols, P(MP), mp_rows, P(),
        ),
        check_vma=False,
    )
```

```python
import functools
import math

import jax
import jax.numpy as jnp
import numpy as np
from jax import lax
from jax.experimental import pallas as pl
from jax.experimental.pallas import tpu as pltpu
from jax.sharding import Mesh
from jax.sharding import PartitionSpec as P

DK = 256
DV = 512
AXES = ("x", "yh", "c", "yl", "z")
DP = ("x", "yh", "c")
MP = ("yl", "z")
BF = jnp.bfloat16
F32 = jnp.float32
MIB = 1024 * 1024

norm_eps = 1e-05
group_eps = 1.0

WAVE_A = ((0, 0), (1, 0), (-1, 0), (0, 1))
WAVE_B = ((2, 0), (1, 1), (-1, 1), (2, 1))
ORDER = WAVE_A + WAVE_B


def after(value, *others):
    return lax.optimization_barrier((value, *others))[0]


class Line:
    def __init__(self):
        self.last = ()

    def hold(self, value):
        return after(value, *self.last) if self.last else value

    def done(self, value):
        self.last = (value,)
        return value

    def wait(self, *values):
        self.last = (*self.last, *values)


def plus(*terms):
    return functools.reduce(lambda u, v: u + v, [t.astype(F32) for t in terms])


def shifted(value, axis, step):
    size = lax.axis_size(axis)
    return lax.ppermute(value, axis, [((i + step) % size, i) for i in range(size)])


def by_sides(value, axis, way):
    size = lax.axis_size(axis)
    names = ("x", "c") if axis == "x" else ("c", axis)

    def flat(c, i):
        return i * 2 + c if axis == "x" else c * size + i

    pairs = []
    for c, step in ((0, way), (1, -way)):
        for i in range(size):
            pairs.append((flat(c, (i + step) % size), flat(c, i)))
    return lax.ppermute(value, names, pairs)


def across(value, axis):
    return by_sides(value, axis, 1)


def across_back(value, axis):
    return by_sides(value, axis, -1)


class Gather:
    def __init__(self, own):
        self.got = got = {(0, 0): own}
        got[1, 0] = shifted(own, "z", 1)
        got[-1, 0] = shifted(own, "z", -1)
        got[0, 1] = shifted(own, "yl", 1)

    def second(self, line):
        got = self.got
        line.wait(got[0, 1], got[1, 0], got[-1, 0])
        got[2, 0] = across(line.done(by_core(line.hold(got[1, 0]), got[-1, 0])), "z")
        got[1, 1] = shifted(got[0, 1], "z", 1)
        got[-1, 1] = shifted(got[0, 1], "z", -1)
        got[2, 1] = shifted(got[2, 0], "yl", 1)

    def wave(self, places):
        return [self.got[p] for p in places]


class LateGather(Gather):
    def __init__(self, own):
        self.got = {(0, 0): own, (0, 1): shifted(own, "yl", 1)}

    def sides(self, line):
        got = self.got
        own, other = line.hold(got[0, 0]), line.hold(got[0, 1])
        got[1, 0] = shifted(own, "z", 1)
        got[-1, 0] = shifted(own, "z", -1)
        got[1, 1] = shifted(other, "z", 1)
        got[-1, 1] = shifted(other, "z", -1)

    def second(self, line):
        got = self.got
        got[2, 0] = across(line.done(by_core(line.hold(got[1, 0]), got[-1, 0])), "z")

    def third(self, line):
        self.got[2, 1] = shifted(line.hold(self.got[2, 0]), "yl", 1)


class Scatter:
    def __init__(self, part):
        self.part = part
        self.far = shifted(part[2, 1], "yl", 1)
        self.up = shifted(part[1, 1], "z", -1)
        self.down = shifted(part[-1, 1], "z", 1)

    def relay(self, line):
        line.wait(self.far)
        self.passed = across_back(line.done(added(line.hold(self.part[2, 0]), self.far)), "z")

    def side(self, line):
        part = self.part
        line.wait(self.up, self.down)
        self.other = shifted(line.done(added(line.hold(part[0, 1]), self.up, self.down)), "yl", 1)

    def near(self, line):
        part = self.part
        line.wait(self.passed)
        up, down = pair(line.hold(part[1, 0]), part[-1, 0], self.passed)
        line.done(up)
        self.near_up = shifted(up, "z", -1)
        self.near_down = shifted(down, "z", 1)

    def terms(self):
        return [self.part[0, 0], self.other, self.near_up, self.near_down]


class Summed:
    def __init__(self, value, axes):
        self.value, self.left, self.come = value, [], None
        for axis in axes:
            size = lax.axis_size(axis)
            mates = ((1, 0),) if size == 2 else ((1, 0, 3, 2), (3, 2, 1, 0))
            self.left += [(axis, [(i, mate[i]) for i in range(size)]) for mate in mates]

    def step(self, line):
        if self.come is not None:
            line.wait(self.come)
            self.value = line.done(line.hold(self.value) + self.come)
            self.come = None
        if self.left:
            axis, pairs = self.left.pop(0)
            self.come = lax.ppermute(self.value, axis, pairs)


def dot_nn(a, b):
    return jnp.dot(a, b, preferred_element_type=F32)


def dot_nt(a, b):
    return lax.dot_general(a, b, (((1,), (1,)), ((), ())), preferred_element_type=F32)


def dot_tn(a, b):
    return lax.dot_general(a, b, (((0,), (0,)), ((), ())), preferred_element_type=F32)


def like(shape, dtype):
    return jax.ShapeDtypeStruct(shape, dtype)


def in_hbm(value):
    return pltpu.with_memory_space_constraint(value, pltpu.HBM)


NO_COST = pl.CostEstimate(flops=0, bytes_accessed=0, transcendentals=0)


def simple(body, outs, args, name, vmem, scalars=0, scratch=()):
    in_specs = [pl.BlockSpec(memory_space=pltpu.SMEM)] * scalars
    in_specs += [pl.BlockSpec(memory_space=pltpu.VMEM)] * (len(args) - scalars)
    return pl.pallas_call(
        body,
        in_specs=in_specs,
        out_specs=[pl.BlockSpec(memory_space=pltpu.VMEM)] * len(outs),
        out_shape=outs,
        scratch_shapes=list(scratch),
        compiler_params=pltpu.CompilerParams(vmem_limit_bytes=vmem * MIB),
        cost_estimate=NO_COST,
        name=name,
    )(*args)


def centred(values):
    centre = values - jnp.mean(values, -1, keepdims=True)
    scale = lax.rsqrt(jnp.mean(centre * centre, -1, keepdims=True) + norm_eps)
    return centre * scale, scale


def norm_kernel(inputs, gain, bias, out):
    xhat, _ = centred(inputs[...].astype(F32))
    out[...] = (xhat * gain[...] + bias[...]).astype(BF)


def norm(inputs, gain, bias):
    return simple(norm_kernel, [like(inputs.shape, BF)], [inputs, gain, bias], "norm", 6)[0]


def middle_kernel(inputs, own, side, up, down, gain, bias, middle, out):
    value = inputs[...].astype(F32) + plus(own[...], side[...], up[...], down[...])
    middle[...] = value
    xhat, _ = centred(value)
    out[...] = (xhat * gain[...] + bias[...]).astype(BF)


def middle_norm(inputs, terms, gain, bias):
    outs = [like(inputs.shape, F32), like(inputs.shape, BF)]
    return simple(middle_kernel, outs, [inputs, *terms, gain, bias], "middle", 10)


def norm_back(xhat, scale, grad, gain):
    e = grad * gain
    return scale * (e - jnp.mean(e, -1, keepdims=True) - xhat * jnp.mean(e * xhat, -1, keepdims=True))


def middle_back_kernel(middle, cot, own, side, up, down, gain, grad, low, sums):
    xhat, scale = centred(middle[...])
    term = plus(own[...], side[...], up[...], down[...])
    dy = cot[...].astype(F32)
    value = dy + norm_back(xhat, scale, term, gain[...])
    grad[...] = value
    low[...] = value.astype(BF)
    sums[0:1, :] = jnp.sum(term * xhat, 0, keepdims=True)
    sums[1:2, :] = jnp.sum(term, 0, keepdims=True)
    sums[2:3, :] = jnp.sum(dy, 0, keepdims=True)


def middle_back(middle, cot, terms, gain):
    outs = [like(middle.shape, F32), like(middle.shape, BF), like((3, middle.shape[1]), F32)]
    return simple(middle_back_kernel, outs, [middle, cot, *terms, gain], "middle_back", 12)


def input_back_kernel(inputs, middle_grad, own, side, up, down, gain, grad, sums):
    xhat, scale = centred(inputs[...].astype(F32))
    term = plus(own[...], side[...], up[...], down[...])
    grad[...] = middle_grad[...] + norm_back(xhat, scale, term, gain[...])
    sums[0:1, :] = jnp.sum(term * xhat, 0, keepdims=True)
    sums[1:2, :] = jnp.sum(term, 0, keepdims=True)


def input_back(inputs, middle_grad, terms, gain):
    outs = [like(inputs.shape, F32), like((2, inputs.shape[1]), F32)]
    return simple(input_back_kernel, outs, [inputs, middle_grad, *terms, gain], "input_back", 12)


def angle_tables(rows, blocks):
    half = DK // 2
    frequency = np.repeat(np.exp(-math.log(10000.0) * np.arange(half) / max(half - 1, 1)), 2)
    inner = np.arange(rows)[:, None] * frequency[None, :]
    outer = (np.arange(blocks) * rows)[:, None] * frequency[None, :]
    return [jnp.asarray(t, F32) for t in (np.cos(inner), np.sin(inner), np.cos(outer), np.sin(outer))]


def turn(values, cosine, sine, back):
    lane = lax.broadcasted_iota(jnp.int32, values.shape, 1)
    even = lane % 2 == 0
    if back:
        turned = values * sine
        return values * cosine + jnp.where(even, pltpu.roll(turned, DK - 1, 1), -pltpu.roll(turned, 1, 1))
    return values * cosine + jnp.where(even, -pltpu.roll(values, DK - 1, 1), pltpu.roll(values, 1, 1)) * sine


def block_angles(marks, number, tables):
    cos_in, sin_in, cos_out, sin_out = tables
    rows = cos_in.shape[0]
    block, first, second = marks[number], marks[8], marks[9]

    def joined(outer, inner):
        co, so = cos_out[pl.ds(outer, 1), :], sin_out[pl.ds(outer, 1), :]
        ci, si = cos_in[inner, :], sin_in[inner, :]
        return ci * co - si * so, si * co + ci * so

    cosine, sine = joined(block, slice(0, rows))
    cos_one, sin_one = joined(0, pl.ds(lax.rem(first, rows), 1))
    last = jnp.minimum(lax.div(second, rows), cos_out.shape[0] - 1)
    cos_two, sin_two = joined(last, pl.ds(lax.rem(second, rows), 1))
    token = block * rows + lax.broadcasted_iota(jnp.int32, (rows, 1), 0)
    back_cos = jnp.where(token >= second, cos_two, jnp.where(token >= first, cos_one, 1.0))
    back_sin = jnp.where(token >= second, sin_two, jnp.where(token >= first, sin_one, 0.0))
    return cosine * back_cos + sine * back_sin, sine * back_cos - cosine * back_sin


def pack(blocks, out):
    rows = blocks[0].shape[0]
    for n, block in enumerate(blocks):
        out[n * rows : (n + 1) * rows, :] = block[...]


def unpack(value, first, outs):
    rows = outs[0].shape[0]
    for n in range(value.shape[0] // rows):
        out = outs[first + n]
        out[...] = value[n * rows : (n + 1) * rows, :].astype(out.dtype)


def heads_kernel(marks, b0, b1, b2, b3, wq, wk, wv, wg, ci, si, co, so, x, qr, kr, vb, gate, *, first):
    pack((b0, b1, b2, b3), x)
    rows = b0.shape[0]
    q = dot_nn(x[...], wq[...])
    k = dot_nn(x[...], wk[...])
    for n in range(4):
        cosine, sine = block_angles(marks, first + n, (ci, si, co, so))
        at = slice(n * rows, (n + 1) * rows)
        qr[at, :] = turn(q[at, :], cosine, sine, False).astype(BF)
        kr[at, :] = turn(k[at, :], cosine, sine, False).astype(BF)
    vb[...] = dot_nn(x[...], wv[...]).astype(BF)
    gate[...] = dot_nn(x[...], wg[...])


def heads(marks, blocks, weights, tables, first):
    rows, width = blocks[0].shape
    n = 4 * rows
    outs = [like((n, width), BF), like((n, DK), BF), like((n, DK), BF), like((n, DV), BF), like((n, DV), F32)]
    return simple(
        functools.partial(heads_kernel, first=first), outs, [marks, *blocks, *weights, *tables], "heads", 20, 1
    )


def places_of(marks, first, rows, axis):
    shape = (rows, 1) if axis == 0 else (1, rows)
    lane = lax.broadcasted_iota(jnp.int32, shape, axis)
    return jnp.concatenate([marks[first + n] * rows + lane for n in range(4)], axis)


def row_marks(marks, decay, first, rows):
    place = places_of(marks, first, rows, 0)
    low = jnp.where(place >= marks[9], marks[9], jnp.where(place >= marks[8], marks[8], 0))
    return place, low, jnp.exp(place.astype(F32) * decay[0])


def col_marks(marks, decay, first, rows):
    place = places_of(marks, first, rows, 1)
    return place, jnp.exp(place.astype(F32) * -decay[0])


def mask_of(at, row, col):
    place, low, fade = (m[at, :] for m in row)
    seen = (col[0] <= place) & (col[0] >= low)
    return jnp.where(seen, fade * col[1], 0.0)


def retain_kernel(
    marks, decay, qr, kr_a, kr_b, vb_a, vb_b, gate, w_out, ret, gated, *outs, first
):
    half = kr_a.shape[0]
    tile = qr.shape[0] // 2
    rows = half // 4
    row = row_marks(marks, decay, first, rows)
    cols = [col_marks(marks, decay, n, rows) for n in (0, 4)]
    for i in range(2):
        at = slice(i * tile, (i + 1) * tile)
        out = None
        for k, v, col in ((kr_a, vb_a, cols[0]), (kr_b, vb_b, cols[1])):
            scores = (dot_nt(qr[at, :], k[...]) * mask_of(at, row, col)).astype(BF)
            term = dot_nn(scores, v[...])
            out = term if out is None else out + term
        ret[at, :] = out
        scale = lax.rsqrt(jnp.mean(out * out, -1, keepdims=True) + group_eps)
        g = gate[at, :]
        low = (g / (1.0 + jnp.exp(-g)) * out * scale).astype(BF)
        gated[at, :] = low
        unpack(dot_nn(low, w_out[...]), i * 2, outs)


def block_outs(places, shape):
    return [like(shape, F32 if p == (0, 0) else BF) for p in places]


def retain(marks, decay, places, q, ks, vs, gate, w_out):
    rows = q.shape[0]
    outs = [like((rows, DV), F32), like((rows, DV), BF)] + block_outs(places, (rows // 4, w_out.shape[1]))
    body = functools.partial(retain_kernel, first=ORDER.index(places[0]))
    got = simple(body, outs, [marks, decay, q, *ks, *vs, gate, w_out], "retain", 16, 2)
    return got[0], got[1], dict(zip(places, got[2:]))


def hidden_grad_kernel(b0, b1, b2, b3, w_down, packed, out):
    pack((b0, b1, b2, b3), packed)
    out[...] = dot_nt(packed[...], w_down[...])


def hidden_grad(blocks, w_down):
    rows, width = blocks[0].shape
    outs = [like((4 * rows, width), BF), like((4 * rows, w_down.shape[0]), F32)]
    return simple(hidden_grad_kernel, outs, [*blocks, w_down], "hidden_grad", 12)


def feed_kernel(b0, b1, b2, b3, w_up, b_up, dh, packed, hidden, dpre, bias_sum, *outs):
    pack((b0, b1, b2, b3), packed)
    tile = packed.shape[0] // 2
    total = None
    for i in range(2):
        at = slice(i * tile, (i + 1) * tile)
        pre = dot_nn(packed[at, :], w_up[...]) + b_up[...]
        below = 0.5 * (1.0 + lax.erf(pre * (1.0 / math.sqrt(2.0))))
        hidden[at, :] = (pre * below).astype(BF)
        slope = below + pre * jnp.exp(-0.5 * pre * pre) * (1.0 / math.sqrt(2.0 * math.pi))
        low = (dh[at, :] * slope).astype(BF)
        dpre[at, :] = low
        column = jnp.sum(low.astype(F32), 0, keepdims=True)
        total = column if total is None else total + column
        unpack(dot_nt(low, w_up[...]), i * 2, outs)
    bias_sum[...] = total


def feed(places, blocks, w_up, b_up, dh):
    rows, width = blocks[0].shape
    hidden = w_up.shape[1]
    n = 4 * rows
    outs = [like((n, width), BF), like((n, hidden), BF), like((n, hidden), BF), like((1, hidden), F32)]
    outs += block_outs(places, (rows, width))
    got = simple(feed_kernel, outs, [*blocks, w_up, b_up, dh], "feed", 16)
    return *got[:4], dict(zip(places, got[4:]))


def feed_out_kernel(hidden, w_down, *outs):
    tile = hidden.shape[0] // 2
    for i in range(2):
        unpack(dot_nn(hidden[i * tile : (i + 1) * tile, :], w_down[...]), i * 2, outs)


def feed_out(places, hidden, w_down):
    outs = block_outs(places, (hidden.shape[0] // 4, w_down.shape[1]))
    return dict(zip(places, simple(feed_out_kernel, outs, [hidden, w_down], "feed_out", 10)))


def gate_back_kernel(b0, b1, b2, b3, w_out, ret, gate, packed, dret, dgate):
    pack((b0, b1, b2, b3), packed)
    tile = packed.shape[0] // 2
    for i in range(2):
        at = slice(i * tile, (i + 1) * tile)
        dgt = dot_nt(packed[at, :], w_out[...])
        g = gate[at, :]
        out = ret[at, :]
        sig = 1.0 / (1.0 + jnp.exp(-g))
        scale = lax.rsqrt(jnp.mean(out * out, -1, keepdims=True) + group_eps)
        y = out * scale
        dgate[at, :] = (dgt * y * (sig * (1.0 + g * (1.0 - sig)))).astype(BF)
        e = dgt * (g * sig)
        dret[at, :] = (scale * (e - y * jnp.mean(e * y, -1, keepdims=True))).astype(BF)


def gate_back(blocks, w_out, ret, gate):
    rows, width = blocks[0].shape
    outs = [like((4 * rows, width), BF), like((4 * rows, DV), BF), like((4 * rows, DV), BF)]
    return simple(gate_back_kernel, outs, [*blocks, w_out, ret, gate], "gate_back", 16)


def retain_back_kernel(
    marks, decay, qr_a, qr_b, kr_a, kr_b, vb_a, vb_b, dret_a, dret_b, ci, si, co, so,
    grads_a, grads_b, dk_sum, dv_sum,
):
    half = qr_a.shape[0]
    tile = half // 2
    rows = ci.shape[0]
    tables = (ci, si, co, so)

    def turned(value, block):
        cosine, sine = block_angles(marks, block, tables)
        return turn(value, cosine, sine, True).astype(BF)

    row_parts = [row_marks(marks, decay, n, rows) for n in (0, 4)]
    col_parts = [col_marks(marks, decay, n, rows) for n in (0, 4)]
    for i in range(4):
        q_ref, dret_ref, grads = (qr_a, dret_a, grads_a) if i < 2 else (qr_b, dret_b, grads_b)
        at = slice(i % 2 * tile, (i % 2 + 1) * tile)
        q = q_ref[at, :]
        dret = dret_ref[at, :]
        dq = None
        for j, (k, v) in enumerate(((kr_a, vb_a), (kr_b, vb_b))):
            cols = slice(j * half, (j + 1) * half)
            mask = mask_of(at, row_parts[i // 2], col_parts[j])
            scores = (dot_nt(q, k[...]) * mask).astype(BF)
            raw = (dot_nt(dret, v[...]) * mask).astype(BF)
            term = dot_nn(raw, k[...])
            dq = term if dq is None else dq + term
            if i == 0:
                dk_sum[cols, :] = dot_tn(raw, q)
                dv_sum[cols, :] = dot_tn(scores, dret)
            else:
                dk_sum[cols, :] += dot_tn(raw, q)
                dv_sum[cols, :] += dot_tn(scores, dret)
        for n in range(tile // rows):
            grads[i % 2 * tile + n * rows : i % 2 * tile + (n + 1) * rows, 0:DK] = turned(
                dq[n * rows : (n + 1) * rows, :], i * (tile // rows) + n
            )
    for j, grads in enumerate((grads_a, grads_b)):
        for n in range(half // rows):
            at = slice(j * half + n * rows, j * half + (n + 1) * rows)
            grads[n * rows : (n + 1) * rows, DK : 2 * DK] = turned(dk_sum[at, :], j * (half // rows) + n)
        grads[:, 2 * DK : 2 * DK + DV] = dv_sum[j * half : (j + 1) * half, :].astype(BF)


def retain_back(marks, decay, qs, ks, vs, drets, tables):
    half = qs[0].shape[0]
    outs = [like((half, 2 * DK + DV), BF)] * 2
    scratch = [pltpu.VMEM((2 * half, DK), F32), pltpu.VMEM((2 * half, DV), F32)]
    args = [marks, decay, *qs, *ks, *vs, *drets, *tables]
    return simple(retain_back_kernel, outs, args, "retain_back", 18, 2, scratch)


def heads_back_kernel(dqkv, dgate, wq, wk, wv, wg, *outs):
    tile = dqkv.shape[0] // 2
    for i in range(2):
        at = slice(i * tile, (i + 1) * tile)
        total = dot_nt(dqkv[at, 0:DK], wq[...]) + dot_nt(dqkv[at, DK : 2 * DK], wk[...])
        total = total + dot_nt(dqkv[at, 2 * DK : 2 * DK + DV], wv[...]) + dot_nt(dgate[at, :], wg[...])
        unpack(total, i * 2, outs)


def heads_back(places, dqkv, dgate, weights):
    outs = block_outs(places, (dqkv.shape[0] // 4, weights[0].shape[0]))
    return dict(zip(places, simple(heads_back_kernel, outs, [dqkv, dgate, *weights], "heads_back", 18)))


def added_kernel(*refs):
    refs[-1][...] = plus(*[r[...] for r in refs[:-1]]).astype(BF)


def added(*terms):
    return simple(added_kernel, [like(terms[0].shape, BF)], list(terms), "added", 6)[0]


def chosen_kernel(core, first, second, out):
    @pl.when(core[0] == 0)
    def _():
        out[...] = first[...]

    @pl.when(core[0] != 0)
    def _():
        out[...] = second[...]


def by_core(first, second):
    core = lax.axis_index("c").astype(jnp.int32)[None]
    return simple(chosen_kernel, [like(first.shape, first.dtype)], [core, first, second], "chosen", 6, 1)[0]


def pair_kernel(core, up, down, passed, new_up, new_down):
    first = core[0] == 0
    value = passed[...].astype(F32)
    new_up[...] = (up[...].astype(F32) + jnp.where(first, value, 0.0)).astype(BF)
    new_down[...] = (down[...].astype(F32) + jnp.where(first, 0.0, value)).astype(BF)


def pair(up, down, passed):
    core = lax.axis_index("c").astype(jnp.int32)[None]
    return simple(pair_kernel, [like(up.shape, BF)] * 2, [core, up, down, passed], "pair", 6, 1)


def near_kernel(near, passed, out):
    rows = passed.shape[0]
    out[0:rows, :] = plus(near[0:rows, :], passed[...]).astype(BF)
    out[rows : 2 * rows, :] = near[rows : 2 * rows, :]


def quarter_kernel(own, come, swapped, out):
    rows = own.shape[0]
    out[...] = plus(own[...], come[0:rows, :], swapped[rows : 2 * rows, :]).astype(BF)


def both_kernel(first, second, out):
    rows = first.shape[0]
    out[0:rows, :] = first[...]
    out[rows : 2 * rows, :] = second[...]


def upper_kernel(both, out):
    out[...] = both[0 : out.shape[0], :]


def weight_kernel(places, *refs, counts, rest):
    refs = list(refs)
    lefts, rights = [], []
    for count in counts:
        lefts.append([refs.pop(0) for _ in range(count)])
        rights.append([refs.pop(0) for _ in range(count)])
    more = refs.pop(0) if rest else None
    step = pl.program_id(0)
    at = 0
    parts = []
    for left, right in zip(lefts, rights):
        total = functools.reduce(lambda u, v: u + v, [dot_tn(l[...], r[...]) for l, r in zip(left, right)])
        width = total.shape[1]
        if rest:
            total = total + more[:, at : at + width].astype(F32)
        parts.append((at, width, total.astype(BF)))
        at += width
    if not rest:
        for at, width, total in parts:
            refs[0][:, at : at + width] = total
        return
    two, near, own = refs
    rows = two.shape[0]
    for k, (out, first) in enumerate(((two, 0), (near, 0), (near, rows), (own, 0))):

        @pl.when(step == k)
        def _(out=out, first=first):
            for at, width, total in parts:
                out[first : first + rows, at : at + width] = total


def weight_parts(pairs, places, first, more):
    piece = pairs[0][0][0].shape[1] // 8
    specs, args, columns = [], [], 0
    for lefts, rights in pairs:
        for left in lefts:
            specs.append(pl.BlockSpec((left.shape[0], piece), lambda i, places: (0, places[first + i])))
            args.append(left)
        for right, shape, at in rights:
            specs.append(pl.BlockSpec(shape, lambda i, places, at=at: at))
            args.append(right)
        columns += rights[0][1][1]
    if more is None:
        out_specs = pl.BlockSpec((piece, columns), lambda i, places: (i, 0))
        out_shape = like((4 * piece, columns), BF)
    else:
        specs.append(pl.BlockSpec((piece, columns), lambda i, places: (i, 0)))
        args.append(more)
        out_shape = [like((piece * n, columns), BF) for n in (1, 2, 1)]
        out_specs = [pl.BlockSpec(o.shape, lambda i, places: (0, 0)) for o in out_shape]
    return pl.pallas_call(
        functools.partial(weight_kernel, counts=[len(lefts) for lefts, _ in pairs], rest=more is not None),
        grid_spec=pltpu.PrefetchScalarGridSpec(num_scalar_prefetch=1, grid=(4,), in_specs=specs, out_specs=out_specs),
        out_shape=out_shape,
        compiler_params=pltpu.CompilerParams(vmem_limit_bytes=16 * MIB),
        cost_estimate=NO_COST,
        name="weight_parts",
    )(places, *args)


def piece_places():
    size = lax.axis_size("x")
    xi = lax.axis_index("x")

    def number(half, step):
        return half * size + (xi + step + size) % size

    def kept(core):
        way = 1 - 2 * core
        return [number(core, 2), number(core, way), number(1 - core, way), number(core, 0)]

    core = lax.axis_index("c")
    way = 1 - 2 * core
    last = [number(core, 0), number(1 - core, 0), number(core, -way), number(1 - core, -way)]
    last += [number(1 - core, way), number(core, way), number(core, 2), number(1 - core, 2)]
    return [jnp.stack(p).astype(jnp.int32) for p in (kept(1 - core) + kept(core), last)]


def holding(line, pairs):
    (lefts, rights), *more = pairs
    return [([line.hold(lefts[0]), *lefts[1:]], rights), *more]


class OverGroups:
    def __init__(self, places):
        self.places = places

    def send(self, line, pairs):
        self.pairs = pairs
        self.other = shifted(line.done(weight_parts(holding(line, pairs), self.places, 0, None)), "c", 1)

    def keep(self, line):
        line.wait(self.other)
        two, self.side, self.own = weight_parts(holding(line, self.pairs), self.places, 4, self.other)
        line.done(self.own)
        self.passed = across_back(two, "x")

    def near(self, line):
        line.wait(self.passed)
        shape = self.side.shape
        side = simple(near_kernel, [like(shape, BF)], [line.hold(self.side), self.passed], "near", 8)[0]
        self.come = across_back(line.done(side), "x")

    def half(self, line):
        line.wait(self.come)
        self.come = line.done(line.hold(self.come))
        self.swapped = shifted(self.come, "c", 1)

    def quarter(self, line):
        line.wait(self.swapped)
        args = [line.hold(self.own), self.come, self.swapped]
        self.mine = line.done(simple(quarter_kernel, [like(self.own.shape, BF)], args, "quarter", 8)[0])
        self.theirs = shifted(self.mine, "yh", 1)

    def whole(self, line):
        line.wait(self.theirs)
        self.mine = line.done(added(line.hold(self.mine), self.theirs))
        self.swapped = shifted(self.mine, "c", 1)

    def spread(self, line):
        line.wait(self.swapped)
        rows, width = self.mine.shape
        args = [line.hold(self.mine), self.swapped]
        self.both = line.done(simple(both_kernel, [like((2 * rows, width), BF)], args, "both", 8)[0])
        self.come = across_back(self.both, "x")

    def last(self, line):
        line.wait(self.come)
        upper = simple(upper_kernel, [like(self.mine.shape, BF)], [line.hold(self.come)], "upper", 6)[0]
        self.two = across_back(line.done(upper), "x")

    def swap(self, line):
        line.wait(self.two)
        come, two = line.hold(self.come), line.hold(self.two)
        self.moved = [shifted(come, "c", 1), shifted(two, "c", 1)]

    def pieces(self, line):
        line.wait(*self.moved)
        return [line.hold(self.both), self.come, self.moved[0], self.two, self.moved[1]]


def place_kernel(places, *refs, columns, turned, counts):
    step = pl.program_id(0)
    pieces, outs = refs[: len(counts)], refs[len(counts) :]
    first = 0
    for piece, count in zip(pieces, counts):

        @pl.when((step >= first) & (step < first + count))
        def _(piece=piece):
            at = 0
            for out, width, turn_it in zip(outs, columns, turned):
                value = piece[:, at : at + width].astype(F32)
                out[...] = value.T if turn_it else value
                at += width

        first += count


def placed(pieces, places, columns, turned):
    rows = min(p.shape[0] for p in pieces)
    counts = [p.shape[0] // rows for p in pieces]
    out_specs, out_shape, in_specs = [], [], []
    for width, turn_it in zip(columns, turned):
        if turn_it:
            out_specs.append(pl.BlockSpec((width, rows), lambda i, places: (0, places[i])))
            out_shape.append(jax.ShapeDtypeStruct((width, 8 * rows), F32))
        else:
            out_specs.append(pl.BlockSpec((rows, width), lambda i, places: (places[i], 0)))
            out_shape.append(jax.ShapeDtypeStruct((8 * rows, width), F32))
    first = 0
    for piece, count in zip(pieces, counts):
        in_specs.append(
            pl.BlockSpec((rows, piece.shape[1]), lambda i, places, f=first, n=count: (jnp.clip(i - f, 0, n - 1), 0))
        )
        first += count
    return pl.pallas_call(
        functools.partial(place_kernel, columns=columns, turned=turned, counts=counts),
        grid_spec=pltpu.PrefetchScalarGridSpec(
            num_scalar_prefetch=1, grid=(8,), in_specs=in_specs, out_specs=out_specs
        ),
        out_shape=out_shape,
        compiler_params=pltpu.CompilerParams(vmem_limit_bytes=16 * MIB),
        cost_estimate=NO_COST,
        name="placed",
    )(places, *pieces)


def local(
    tokens_in,
    cotangent,
    lengths,
    ln1_gain,
    ln1_bias,
    w_query,
    w_key,
    w_value,
    w_gate,
    w_out,
    ln2_gain,
    ln2_bias,
    w_up,
    b_up,
    w_down,
    b_down,
):
    rows = tokens_in.shape[0]
    half = rows * 4
    z_size = lax.axis_size("z")
    blocks = z_size * lax.axis_size("yl")
    zi = lax.axis_index("z")
    yi = lax.axis_index("yl")
    ends = jnp.cumsum(lengths[0])
    marks = [((yi + dy) % 2) * z_size + (zi + dz) % z_size for dz, dy in ORDER] + [ends[0], ends[1]]
    marks = jnp.stack([m.astype(jnp.int32) for m in marks])
    decay = jnp.log1p(-jnp.exp2(-5.0 - lax.axis_index(MP).astype(F32)))[None]
    tables = angle_tables(rows, blocks)
    places, final = piece_places()
    weights = (w_query, w_key, w_value, w_gate)
    heads_weights = tuple(in_hbm(w) for w in weights)
    gain_one, bias_one, gain_two, bias_two = (v[None, :] for v in (ln1_gain, ln1_bias, ln2_gain, ln2_bias))
    square = (half, DV)
    line = Line()

    xg = Gather(line.done(norm(tokens_in, gain_one, bias_one)))
    cg = LateGather(line.hold(cotangent))
    line.done(marks)
    xg.second(line)
    got = xg.got
    line.wait(got[2, 0], cg.got[0, 1])
    cg.sides(line)
    x_a, q_a, k_a, v_a, gate_a = heads(
        marks, [line.hold(got[0, 0]), got[1, 0], got[-1, 0], got[0, 1]], heads_weights, tables, 0
    )
    line.done(q_a)
    line.wait(got[1, 1], got[-1, 1], got[2, 1])
    x_b, q_b, k_b, v_b, gate_b = heads(
        marks, [line.hold(got[2, 0])] + xg.wave(WAVE_B[1:]), heads_weights, tables, 4
    )
    line.done(q_b)
    ks, vs = (k_a, k_b), (v_a, v_b)
    ret_b, gated_b, part_b = retain(marks, decay, WAVE_B, q_b, ks, vs, gate_b, w_out)
    line.done(gated_b)
    cot = cg.got
    line.wait(cot[1, 0], cot[-1, 0], cot[1, 1], cot[-1, 1])
    ret_a, gated_a, part_a = retain(marks, decay, WAVE_A, line.hold(q_a), ks, vs, gate_a, w_out)
    line.done(gated_a)
    rs = Scatter({**part_a, **part_b})
    rs.relay(line)
    rs.side(line)
    cg.second(line)
    rs.near(line)
    cot_a, dh_a = hidden_grad([line.hold(cot[0, 0])] + cg.wave(WAVE_A[1:]), w_down)
    line.done(dh_a)
    line.wait(cot[2, 0])
    cg.third(line)
    first, *others = rs.terms()
    line.wait(*others)
    middle, normed_two = middle_norm(tokens_in, [line.hold(first), *others], gain_two, bias_two)

    ng = Gather(line.done(normed_two))
    line.wait(cot[2, 1])
    cot_b, dh_b = hidden_grad([line.hold(cot[2, 0])] + cg.wave(WAVE_B[1:]), w_down)
    line.done(dh_b)
    ng.second(line)
    got = ng.got
    line.wait(got[2, 0])
    n_a, hid_a, dpre_a, bsum_a, part_a = feed(
        WAVE_A, [line.hold(got[0, 0]), got[1, 0], got[-1, 0], got[0, 1]], w_up, b_up[None, :], dh_a
    )
    line.done(bsum_a)
    line.wait(got[1, 1], got[-1, 1], got[2, 1])
    n_b, hid_b, dpre_b, bsum_b, part_b = feed(
        WAVE_B, [line.hold(got[2, 0])] + ng.wave(WAVE_B[1:]), w_up, b_up[None, :], dh_b
    )
    line.done(bsum_b)
    rs = Scatter({**part_a, **part_b})
    out_b = feed_out(WAVE_B, line.hold(hid_b), w_down)
    line.done(out_b[2, 1])
    out_a = feed_out(WAVE_A, line.hold(hid_a), w_down)
    line.done(out_a[0, 1])
    rs.relay(line)
    rs.side(line)
    feed_sums = OverGroups(places)
    feed_sums.send(
        line,
        [
            ([n_a, n_b], [(dpre_a, dpre_a.shape, (0, 0)), (dpre_b, dpre_b.shape, (0, 0))]),
            ([cot_a, cot_b], [(hid_a, hid_a.shape, (0, 0)), (hid_b, hid_b.shape, (0, 0))]),
        ],
    )
    rs.near(line)
    feed_sums.keep(line)
    first, *others = rs.terms()
    line.wait(*others)
    grad_middle, branch, early = middle_back(middle, cotangent, [line.hold(first), *others], gain_two)

    bg = Gather(line.done(branch))
    feed_sums.near(line)
    bg.second(line)
    got = bg.got
    line.wait(got[2, 0])
    br_a, dret_a, dgate_a = gate_back(
        [line.hold(got[0, 0]), got[1, 0], got[-1, 0], got[0, 1]], w_out, ret_a, gate_a
    )
    line.done(dret_a)
    feed_sums.half(line)
    feed_sums.quarter(line)
    line.wait(got[1, 1], got[-1, 1], got[2, 1])
    br_b, dret_b, dgate_b = gate_back([line.hold(got[2, 0])] + bg.wave(WAVE_B[1:]), w_out, ret_b, gate_b)
    line.done(dret_b)
    gate_sums = OverGroups(places)
    gate_sums.send(
        line,
        [
            ([x_a, x_b], [(dgate_a, square, (0, 0)), (dgate_b, square, (0, 0))]),
            ([br_a, br_b], [(gated_a, square, (0, 0)), (gated_b, square, (0, 0))]),
        ],
    )
    dqkv_a, dqkv_b = retain_back(marks, decay, (q_a, q_b), ks, vs, (line.hold(dret_a), dret_b), tables)
    line.done(dqkv_b)
    gate_sums.keep(line)
    feed_sums.whole(line)
    part_b = heads_back(WAVE_B, line.hold(dqkv_b), dgate_b, weights)
    line.done(part_b[2, 1])
    part_a = heads_back(WAVE_A, line.hold(dqkv_a), dgate_a, weights)
    line.done(part_a[0, 1])
    rs = Scatter({**part_a, **part_b})
    gate_sums.near(line)
    head_sums = OverGroups(places)
    head_sums.send(line, [([x_a, x_b], [(dqkv_a, dqkv_a.shape, (0, 0)), (dqkv_b, dqkv_b.shape, (0, 0))])])
    rs.relay(line)
    rs.side(line)
    head_sums.keep(line)
    gate_sums.half(line)
    gate_sums.quarter(line)
    rs.near(line)
    head_sums.near(line)
    line.wait(rs.other)
    first, *others = rs.terms()
    line.wait(*others)
    grad_x, late = input_back(tokens_in, grad_middle, [line.hold(first), *others], gain_one)
    line.done(late)
    sums = Summed(line.done(jnp.concatenate([late, early], 0)), ("z", "yl"))
    gate_sums.whole(line)
    gate_sums.spread(line)
    sums.step(line)
    head_sums.half(line)
    head_sums.quarter(line)
    sums.step(line)
    sums.step(line)
    gate_sums.last(line)
    feed_sums.spread(line)
    head_sums.whole(line)
    head_sums.spread(line)
    sums.step(line)
    wide = jnp.pad(bsum_a + bsum_b, ((0, 0), (0, early.shape[1] - bsum_a.shape[1])))
    sums = Summed(line.done(jnp.concatenate([line.hold(sums.value), wide], 0)), ("c", "yh", "x"))
    sums.step(line)
    out_rs = Scatter({**out_a, **{p: line.hold(v) for p, v in out_b.items()}})
    gate_sums.swap(line)
    sums.step(line)
    feed_sums.last(line)
    gate_pieces = [in_hbm(p) for p in gate_sums.pieces(line)]
    grad_gate, grad_out = placed(gate_pieces, final, (DV, DV), (False, True))
    line.done(grad_gate)
    head_sums.last(line)
    out_rs.relay(line)
    out_rs.side(line)
    feed_sums.swap(line)
    grad_up, grad_down = placed(feed_sums.pieces(line), final, (w_up.shape[1], w_down.shape[0]), (False, True))
    line.done(grad_up)
    out_rs.near(line)
    sums.step(line)
    head_sums.swap(line)
    sums.step(line)
    grad_query, grad_key, grad_value = placed(head_sums.pieces(line), final, (DK, DK, DV), (False, False, False))
    sums.step(line)
    line.wait(grad_query)
    sums = sums.value
    b_up_sum = sums[5, : bsum_a.shape[1]]
    first, *others = out_rs.terms()
    result = middle + plus(line.hold(first), *others) + b_down
    return (
        result.astype(BF),
        grad_x,
        sums[0],
        sums[1],
        grad_query,
        grad_key,
        grad_value,
        grad_gate,
        grad_out,
        sums[2],
        sums[3],
        grad_up,
        b_up_sum,
        grad_down,
        sums[4],
    )


def solution(mesh):
    split = Mesh(mesh.devices.reshape(4, 2, 2, 2, 4), AXES)
    rows = P(AXES, None)
    cols = P(None, MP)
    mp_rows = P(MP, None)
    return jax.shard_map(
        local,
        mesh=split,
        in_specs=(
            rows, rows, P(DP, None), P(), P(), cols, cols, cols, cols, mp_rows, P(), P(), cols, P(MP), mp_rows, P(),
        ),
        out_specs=(
            rows, rows, P(), P(), cols, cols, cols, cols, mp_rows, P(), P(), cols, P(MP), mp_rows, P(),
        ),
        check_vma=False,
    )
```

```python
import functools
import math

import jax
import jax.numpy as jnp
import numpy as np
from jax import lax
from jax.experimental import pallas as pl
from jax.experimental.pallas import tpu as pltpu
from jax.sharding import Mesh
from jax.sharding import PartitionSpec as P

DK = 256
DV = 512
AXES = ("x", "yh", "c", "yl", "z")
DP = ("x", "yh", "c")
MP = ("yl", "z")
BF = jnp.bfloat16
F32 = jnp.float32
MIB = 1024 * 1024

norm_eps = 1e-05
group_eps = 1.0

WAVE_A = ((0, 0), (1, 0), (-1, 0), (0, 1))
WAVE_B = ((2, 0), (1, 1), (-1, 1), (2, 1))
ORDER = WAVE_A + WAVE_B


def after(value, *others):
    return lax.optimization_barrier((value, *others))[0]


class Line:
    def __init__(self):
        self.last = ()

    def hold(self, value):
        return after(value, *self.last) if self.last else value

    def done(self, value):
        self.last = (value,)
        return value

    def wait(self, *values):
        self.last = (*self.last, *values)


def plus(*terms):
    return functools.reduce(lambda u, v: u + v, [t.astype(F32) for t in terms])


def shifted(value, axis, step):
    size = lax.axis_size(axis)
    return lax.ppermute(value, axis, [((i + step) % size, i) for i in range(size)])


def by_sides(value, axis, way):
    size = lax.axis_size(axis)
    names = ("x", "c") if axis == "x" else ("c", axis)

    def flat(c, i):
        return i * 2 + c if axis == "x" else c * size + i

    pairs = []
    for c, step in ((0, way), (1, -way)):
        for i in range(size):
            pairs.append((flat(c, (i + step) % size), flat(c, i)))
    return lax.ppermute(value, names, pairs)


def across(value, axis):
    return by_sides(value, axis, 1)


def across_back(value, axis):
    return by_sides(value, axis, -1)


class Gather:
    def __init__(self, own):
        self.got = got = {(0, 0): own}
        got[1, 0] = shifted(own, "z", 1)
        got[-1, 0] = shifted(own, "z", -1)
        got[0, 1] = shifted(own, "yl", 1)

    def second(self, line):
        got = self.got
        line.wait(got[0, 1], got[1, 0], got[-1, 0])
        got[2, 0] = across(line.done(by_core(line.hold(got[1, 0]), got[-1, 0])), "z")
        got[1, 1] = shifted(got[0, 1], "z", 1)
        got[-1, 1] = shifted(got[0, 1], "z", -1)
        got[2, 1] = shifted(got[2, 0], "yl", 1)

    def wave(self, places):
        return [self.got[p] for p in places]


class LateGather(Gather):
    def __init__(self, own):
        self.got = {(0, 0): own, (0, 1): shifted(own, "yl", 1)}

    def sides(self, line):
        got = self.got
        own, other = line.hold(got[0, 0]), line.hold(got[0, 1])
        got[1, 0] = shifted(own, "z", 1)
        got[-1, 0] = shifted(own, "z", -1)
        got[1, 1] = shifted(other, "z", 1)
        got[-1, 1] = shifted(other, "z", -1)

    def second(self, line):
        got = self.got
        got[2, 0] = across(line.done(by_core(line.hold(got[1, 0]), got[-1, 0])), "z")

    def third(self, line):
        self.got[2, 1] = shifted(line.hold(self.got[2, 0]), "yl", 1)


class Scatter:
    def __init__(self, part):
        self.part = part
        self.far = shifted(part[2, 1], "yl", 1)
        self.up = shifted(part[1, 1], "z", -1)
        self.down = shifted(part[-1, 1], "z", 1)

    def relay(self, line):
        line.wait(self.far)
        self.passed = across_back(line.done(added(line.hold(self.part[2, 0]), self.far)), "z")

    def side(self, line):
        part = self.part
        line.wait(self.up, self.down)
        self.other = shifted(line.done(added(line.hold(part[0, 1]), self.up, self.down)), "yl", 1)

    def near(self, line):
        part = self.part
        line.wait(self.passed)
        up, down = pair(line.hold(part[1, 0]), part[-1, 0], self.passed)
        line.done(up)
        self.near_up = shifted(up, "z", -1)
        self.near_down = shifted(down, "z", 1)

    def terms(self):
        return [self.part[0, 0], self.other, self.near_up, self.near_down]


class Summed:
    def __init__(self, value, axes):
        self.value, self.left, self.come = value, [], None
        for axis in axes:
            size = lax.axis_size(axis)
            mates = ((1, 0),) if size == 2 else ((1, 0, 3, 2), (3, 2, 1, 0))
            self.left += [(axis, [(i, mate[i]) for i in range(size)]) for mate in mates]

    def step(self, line):
        if self.come is not None:
            line.wait(self.come)
            self.value = line.done(line.hold(self.value) + self.come)
            self.come = None
        if self.left:
            axis, pairs = self.left.pop(0)
            self.come = lax.ppermute(self.value, axis, pairs)


def dot_nn(a, b):
    return jnp.dot(a, b, preferred_element_type=F32)


def dot_nt(a, b):
    return lax.dot_general(a, b, (((1,), (1,)), ((), ())), preferred_element_type=F32)


def dot_tn(a, b):
    return lax.dot_general(a, b, (((0,), (0,)), ((), ())), preferred_element_type=F32)


def like(shape, dtype):
    return jax.ShapeDtypeStruct(shape, dtype)


def in_hbm(value):
    return pltpu.with_memory_space_constraint(value, pltpu.HBM)


NO_COST = pl.CostEstimate(flops=0, bytes_accessed=0, transcendentals=0)


def simple(body, outs, args, name, vmem, scalars=0, scratch=()):
    in_specs = [pl.BlockSpec(memory_space=pltpu.SMEM)] * scalars
    in_specs += [pl.BlockSpec(memory_space=pltpu.VMEM)] * (len(args) - scalars)
    return pl.pallas_call(
        body,
        in_specs=in_specs,
        out_specs=[pl.BlockSpec(memory_space=pltpu.VMEM)] * len(outs),
        out_shape=outs,
        scratch_shapes=list(scratch),
        compiler_params=pltpu.CompilerParams(vmem_limit_bytes=vmem * MIB),
        cost_estimate=NO_COST,
        name=name,
    )(*args)


def centred(values):
    centre = values - jnp.mean(values, -1, keepdims=True)
    scale = lax.rsqrt(jnp.mean(centre * centre, -1, keepdims=True) + norm_eps)
    return centre * scale, scale


def norm_kernel(inputs, gain, bias, out):
    xhat, _ = centred(inputs[...].astype(F32))
    out[...] = (xhat * gain[...] + bias[...]).astype(BF)


def norm(inputs, gain, bias):
    return simple(norm_kernel, [like(inputs.shape, BF)], [inputs, gain, bias], "norm", 6)[0]


def middle_kernel(inputs, own, side, up, down, gain, bias, middle, out):
    value = inputs[...].astype(F32) + plus(own[...], side[...], up[...], down[...])
    middle[...] = value
    xhat, _ = centred(value)
    out[...] = (xhat * gain[...] + bias[...]).astype(BF)


def middle_norm(inputs, terms, gain, bias):
    outs = [like(inputs.shape, F32), like(inputs.shape, BF)]
    return simple(middle_kernel, outs, [inputs, *terms, gain, bias], "middle", 10)


def norm_back(xhat, scale, grad, gain):
    e = grad * gain
    return scale * (e - jnp.mean(e, -1, keepdims=True) - xhat * jnp.mean(e * xhat, -1, keepdims=True))


def middle_back_kernel(middle, cot, own, side, up, down, gain, grad, low, sums):
    xhat, scale = centred(middle[...])
    term = plus(own[...], side[...], up[...], down[...])
    dy = cot[...].astype(F32)
    value = dy + norm_back(xhat, scale, term, gain[...])
    grad[...] = value
    low[...] = value.astype(BF)
    sums[0:1, :] = jnp.sum(term * xhat, 0, keepdims=True)
    sums[1:2, :] = jnp.sum(term, 0, keepdims=True)
    sums[2:3, :] = jnp.sum(dy, 0, keepdims=True)


def middle_back(middle, cot, terms, gain):
    outs = [like(middle.shape, F32), like(middle.shape, BF), like((3, middle.shape[1]), F32)]
    return simple(middle_back_kernel, outs, [middle, cot, *terms, gain], "middle_back", 12)


def input_back_kernel(inputs, middle_grad, own, side, up, down, gain, grad, sums):
    xhat, scale = centred(inputs[...].astype(F32))
    term = plus(own[...], side[...], up[...], down[...])
    grad[...] = middle_grad[...] + norm_back(xhat, scale, term, gain[...])
    sums[0:1, :] = jnp.sum(term * xhat, 0, keepdims=True)
    sums[1:2, :] = jnp.sum(term, 0, keepdims=True)


def input_back(inputs, middle_grad, terms, gain):
    outs = [like(inputs.shape, F32), like((2, inputs.shape[1]), F32)]
    return simple(input_back_kernel, outs, [inputs, middle_grad, *terms, gain], "input_back", 12)


def angle_tables(rows, blocks):
    half = DK // 2
    frequency = np.repeat(np.exp(-math.log(10000.0) * np.arange(half) / max(half - 1, 1)), 2)
    inner = np.arange(rows)[:, None] * frequency[None, :]
    outer = (np.arange(blocks) * rows)[:, None] * frequency[None, :]
    return [jnp.asarray(t, F32) for t in (np.cos(inner), np.sin(inner), np.cos(outer), np.sin(outer))]


def turn(values, cosine, sine, back):
    lane = lax.broadcasted_iota(jnp.int32, values.shape, 1)
    even = lane % 2 == 0
    if back:
        turned = values * sine
        return values * cosine + jnp.where(even, pltpu.roll(turned, DK - 1, 1), -pltpu.roll(turned, 1, 1))
    return values * cosine + jnp.where(even, -pltpu.roll(values, DK - 1, 1), pltpu.roll(values, 1, 1)) * sine


def block_angles(marks, number, tables):
    cos_in, sin_in, cos_out, sin_out = tables
    rows = cos_in.shape[0]
    block, first, second = marks[number], marks[8], marks[9]

    def joined(outer, inner):
        co, so = cos_out[pl.ds(outer, 1), :], sin_out[pl.ds(outer, 1), :]
        ci, si = cos_in[inner, :], sin_in[inner, :]
        return ci * co - si * so, si * co + ci * so

    cosine, sine = joined(block, slice(0, rows))
    cos_one, sin_one = joined(0, pl.ds(lax.rem(first, rows), 1))
    last = jnp.minimum(lax.div(second, rows), cos_out.shape[0] - 1)
    cos_two, sin_two = joined(last, pl.ds(lax.rem(second, rows), 1))
    token = block * rows + lax.broadcasted_iota(jnp.int32, (rows, 1), 0)
    back_cos = jnp.where(token >= second, cos_two, jnp.where(token >= first, cos_one, 1.0))
    back_sin = jnp.where(token >= second, sin_two, jnp.where(token >= first, sin_one, 0.0))
    return cosine * back_cos + sine * back_sin, sine * back_cos - cosine * back_sin


def pack(blocks, out):
    rows = blocks[0].shape[0]
    for n, block in enumerate(blocks):
        out[n * rows : (n + 1) * rows, :] = block[...]


def unpack(value, first, outs):
    rows = outs[0].shape[0]
    for n in range(value.shape[0] // rows):
        out = outs[first + n]
        out[...] = value[n * rows : (n + 1) * rows, :].astype(out.dtype)


def heads_kernel(marks, b0, b1, b2, b3, wq, wk, wv, wg, ci, si, co, so, x, qr, kr, vb, gate, *, first):
    pack((b0, b1, b2, b3), x)
    rows = b0.shape[0]
    q = dot_nn(x[...], wq[...])
    k = dot_nn(x[...], wk[...])
    for n in range(4):
        cosine, sine = block_angles(marks, first + n, (ci, si, co, so))
        at = slice(n * rows, (n + 1) * rows)
        qr[at, :] = turn(q[at, :], cosine, sine, False).astype(BF)
        kr[at, :] = turn(k[at, :], cosine, sine, False).astype(BF)
    vb[...] = dot_nn(x[...], wv[...]).astype(BF)
    gate[...] = dot_nn(x[...], wg[...])


def heads(marks, blocks, weights, tables, first):
    rows, width = blocks[0].shape
    n = 4 * rows
    outs = [like((n, width), BF), like((n, DK), BF), like((n, DK), BF), like((n, DV), BF), like((n, DV), F32)]
    return simple(
        functools.partial(heads_kernel, first=first), outs, [marks, *blocks, *weights, *tables], "heads", 20, 1
    )


def places_of(marks, first, rows, axis):
    shape = (rows, 1) if axis == 0 else (1, rows)
    lane = lax.broadcasted_iota(jnp.int32, shape, axis)
    return jnp.concatenate([marks[first + n] * rows + lane for n in range(4)], axis)


def row_marks(marks, decay, first, rows):
    place = places_of(marks, first, rows, 0)
    low = jnp.where(place >= marks[9], marks[9], jnp.where(place >= marks[8], marks[8], 0))
    return place, low, jnp.exp(place.astype(F32) * decay[0])


def col_marks(marks, decay, first, rows):
    place = places_of(marks, first, rows, 1)
    return place, jnp.exp(place.astype(F32) * -decay[0])


def mask_of(at, row, col):
    place, low, fade = (m[at, :] for m in row)
    seen = (col[0] <= place) & (col[0] >= low)
    return jnp.where(seen, fade * col[1], 0.0)


def retain_kernel(
    marks, decay, qr, kr_a, kr_b, vb_a, vb_b, gate, w_out, ret, gated, *outs, first
):
    half = kr_a.shape[0]
    tile = qr.shape[0] // 2
    rows = half // 4
    row = row_marks(marks, decay, first, rows)
    cols = [col_marks(marks, decay, n, rows) for n in (0, 4)]
    for i in range(2):
        at = slice(i * tile, (i + 1) * tile)
        out = None
        for k, v, col in ((kr_a, vb_a, cols[0]), (kr_b, vb_b, cols[1])):
            scores = (dot_nt(qr[at, :], k[...]) * mask_of(at, row, col)).astype(BF)
            term = dot_nn(scores, v[...])
            out = term if out is None else out + term
        ret[at, :] = out
        scale = lax.rsqrt(jnp.mean(out * out, -1, keepdims=True) + group_eps)
        g = gate[at, :]
        low = (g / (1.0 + jnp.exp(-g)) * out * scale).astype(BF)
        gated[at, :] = low
        unpack(dot_nn(low, w_out[...]), i * 2, outs)


def block_outs(places, shape):
    return [like(shape, F32 if p == (0, 0) else BF) for p in places]


def retain(marks, decay, places, q, ks, vs, gate, w_out):
    rows = q.shape[0]
    outs = [like((rows, DV), F32), like((rows, DV), BF)] + block_outs(places, (rows // 4, w_out.shape[1]))
    body = functools.partial(retain_kernel, first=ORDER.index(places[0]))
    got = simple(body, outs, [marks, decay, q, *ks, *vs, gate, w_out], "retain", 16, 2)
    return got[0], got[1], dict(zip(places, got[2:]))


def hidden_grad_kernel(b0, b1, b2, b3, w_down, packed, out):
    pack((b0, b1, b2, b3), packed)
    out[...] = dot_nt(packed[...], w_down[...])


def hidden_grad(blocks, w_down):
    rows, width = blocks[0].shape
    outs = [like((4 * rows, width), BF), like((4 * rows, w_down.shape[0]), F32)]
    return simple(hidden_grad_kernel, outs, [*blocks, w_down], "hidden_grad", 12)


def feed_kernel(b0, b1, b2, b3, w_up, b_up, dh, packed, hidden, dpre, bias_sum, *outs):
    pack((b0, b1, b2, b3), packed)
    tile = packed.shape[0] // 2
    total = None
    for i in range(2):
        at = slice(i * tile, (i + 1) * tile)
        pre = dot_nn(packed[at, :], w_up[...]) + b_up[...]
        below = 0.5 * (1.0 + lax.erf(pre * (1.0 / math.sqrt(2.0))))
        hidden[at, :] = (pre * below).astype(BF)
        slope = below + pre * jnp.exp(-0.5 * pre * pre) * (1.0 / math.sqrt(2.0 * math.pi))
        low = (dh[at, :] * slope).astype(BF)
        dpre[at, :] = low
        column = jnp.sum(low.astype(F32), 0, keepdims=True)
        total = column if total is None else total + column
        unpack(dot_nt(low, w_up[...]), i * 2, outs)
    bias_sum[...] = total


def feed(places, blocks, w_up, b_up, dh):
    rows, width = blocks[0].shape
    hidden = w_up.shape[1]
    n = 4 * rows
    outs = [like((n, width), BF), like((n, hidden), BF), like((n, hidden), BF), like((1, hidden), F32)]
    outs += block_outs(places, (rows, width))
    got = simple(feed_kernel, outs, [*blocks, w_up, b_up, dh], "feed", 16)
    return *got[:4], dict(zip(places, got[4:]))


def feed_out_kernel(hidden, w_down, *outs):
    tile = hidden.shape[0] // 2
    for i in range(2):
        unpack(dot_nn(hidden[i * tile : (i + 1) * tile, :], w_down[...]), i * 2, outs)


def feed_out(places, hidden, w_down):
    outs = block_outs(places, (hidden.shape[0] // 4, w_down.shape[1]))
    return dict(zip(places, simple(feed_out_kernel, outs, [hidden, w_down], "feed_out", 10)))


def gate_back_kernel(b0, b1, b2, b3, w_out, ret, gate, packed, dret, dgate):
    pack((b0, b1, b2, b3), packed)
    tile = packed.shape[0] // 2
    for i in range(2):
        at = slice(i * tile, (i + 1) * tile)
        dgt = dot_nt(packed[at, :], w_out[...])
        g = gate[at, :]
        out = ret[at, :]
        sig = 1.0 / (1.0 + jnp.exp(-g))
        scale = lax.rsqrt(jnp.mean(out * out, -1, keepdims=True) + group_eps)
        y = out * scale
        dgate[at, :] = (dgt * y * (sig * (1.0 + g * (1.0 - sig)))).astype(BF)
        e = dgt * (g * sig)
        dret[at, :] = (scale * (e - y * jnp.mean(e * y, -1, keepdims=True))).astype(BF)


def gate_back(blocks, w_out, ret, gate):
    rows, width = blocks[0].shape
    outs = [like((4 * rows, width), BF), like((4 * rows, DV), BF), like((4 * rows, DV), BF)]
    return simple(gate_back_kernel, outs, [*blocks, w_out, ret, gate], "gate_back", 16)


def retain_back_kernel(
    marks, decay, qr_a, qr_b, kr_a, kr_b, vb_a, vb_b, dret_a, dret_b, ci, si, co, so,
    grads_a, grads_b, dk_sum, dv_sum,
):
    half = qr_a.shape[0]
    tile = half // 2
    rows = ci.shape[0]
    tables = (ci, si, co, so)

    def turned(value, block):
        cosine, sine = block_angles(marks, block, tables)
        return turn(value, cosine, sine, True).astype(BF)

    row_parts = [row_marks(marks, decay, n, rows) for n in (0, 4)]
    col_parts = [col_marks(marks, decay, n, rows) for n in (0, 4)]
    for i in range(4):
        q_ref, dret_ref, grads = (qr_a, dret_a, grads_a) if i < 2 else (qr_b, dret_b, grads_b)
        at = slice(i % 2 * tile, (i % 2 + 1) * tile)
        q = q_ref[at, :]
        dret = dret_ref[at, :]
        dq = None
        for j, (k, v) in enumerate(((kr_a, vb_a), (kr_b, vb_b))):
            cols = slice(j * half, (j + 1) * half)
            mask = mask_of(at, row_parts[i // 2], col_parts[j])
            scores = (dot_nt(q, k[...]) * mask).astype(BF)
            raw = (dot_nt(dret, v[...]) * mask).astype(BF)
            term = dot_nn(raw, k[...])
            dq = term if dq is None else dq + term
            if i == 0:
                dk_sum[cols, :] = dot_tn(raw, q)
                dv_sum[cols, :] = dot_tn(scores, dret)
            else:
                dk_sum[cols, :] += dot_tn(raw, q)
                dv_sum[cols, :] += dot_tn(scores, dret)
        for n in range(tile // rows):
            grads[i % 2 * tile + n * rows : i % 2 * tile + (n + 1) * rows, 0:DK] = turned(
                dq[n * rows : (n + 1) * rows, :], i * (tile // rows) + n
            )
    for j, grads in enumerate((grads_a, grads_b)):
        for n in range(half // rows):
            at = slice(j * half + n * rows, j * half + (n + 1) * rows)
            grads[n * rows : (n + 1) * rows, DK : 2 * DK] = turned(dk_sum[at, :], j * (half // rows) + n)
        grads[:, 2 * DK : 2 * DK + DV] = dv_sum[j * half : (j + 1) * half, :].astype(BF)


def retain_back(marks, decay, qs, ks, vs, drets, tables):
    half = qs[0].shape[0]
    outs = [like((half, 2 * DK + DV), BF)] * 2
    scratch = [pltpu.VMEM((2 * half, DK), F32), pltpu.VMEM((2 * half, DV), F32)]
    args = [marks, decay, *qs, *ks, *vs, *drets, *tables]
    return simple(retain_back_kernel, outs, args, "retain_back", 18, 2, scratch)


def heads_back_kernel(dqkv, dgate, wq, wk, wv, wg, *outs):
    tile = dqkv.shape[0] // 2
    for i in range(2):
        at = slice(i * tile, (i + 1) * tile)
        total = dot_nt(dqkv[at, 0:DK], wq[...]) + dot_nt(dqkv[at, DK : 2 * DK], wk[...])
        total = total + dot_nt(dqkv[at, 2 * DK : 2 * DK + DV], wv[...]) + dot_nt(dgate[at, :], wg[...])
        unpack(total, i * 2, outs)


def heads_back(places, dqkv, dgate, weights):
    outs = block_outs(places, (dqkv.shape[0] // 4, weights[0].shape[0]))
    return dict(zip(places, simple(heads_back_kernel, outs, [dqkv, dgate, *weights], "heads_back", 18)))


def added_kernel(*refs):
    refs[-1][...] = plus(*[r[...] for r in refs[:-1]]).astype(BF)


def added(*terms):
    return simple(added_kernel, [like(terms[0].shape, BF)], list(terms), "added", 6)[0]


def chosen_kernel(core, first, second, out):
    @pl.when(core[0] == 0)
    def _():
        out[...] = first[...]

    @pl.when(core[0] != 0)
    def _():
        out[...] = second[...]


def by_core(first, second):
    core = lax.axis_index("c").astype(jnp.int32)[None]
    return simple(chosen_kernel, [like(first.shape, first.dtype)], [core, first, second], "chosen", 6, 1)[0]


def pair_kernel(core, up, down, passed, new_up, new_down):
    first = core[0] == 0
    value = passed[...].astype(F32)
    new_up[...] = (up[...].astype(F32) + jnp.where(first, value, 0.0)).astype(BF)
    new_down[...] = (down[...].astype(F32) + jnp.where(first, 0.0, value)).astype(BF)


def pair(up, down, passed):
    core = lax.axis_index("c").astype(jnp.int32)[None]
    return simple(pair_kernel, [like(up.shape, BF)] * 2, [core, up, down, passed], "pair", 6, 1)


def near_kernel(near, passed, out):
    rows = passed.shape[0]
    out[0:rows, :] = plus(near[0:rows, :], passed[...]).astype(BF)
    out[rows : 2 * rows, :] = near[rows : 2 * rows, :]


def quarter_kernel(own, come, swapped, out):
    rows = own.shape[0]
    out[...] = plus(own[...], come[0:rows, :], swapped[rows : 2 * rows, :]).astype(BF)


def both_kernel(first, second, out):
    rows = first.shape[0]
    out[0:rows, :] = first[...]
    out[rows : 2 * rows, :] = second[...]


def upper_kernel(both, out):
    out[...] = both[0 : out.shape[0], :]


def weight_kernel(places, *refs, counts, rest):
    refs = list(refs)
    lefts, rights = [], []
    for count in counts:
        lefts.append([refs.pop(0) for _ in range(count)])
        rights.append([refs.pop(0) for _ in range(count)])
    more = refs.pop(0) if rest else None
    step = pl.program_id(0)
    at = 0
    parts = []
    for left, right in zip(lefts, rights):
        total = functools.reduce(lambda u, v: u + v, [dot_tn(l[...], r[...]) for l, r in zip(left, right)])
        width = total.shape[1]
        if rest:
            total = total + more[:, at : at + width].astype(F32)
        parts.append((at, width, total.astype(BF)))
        at += width
    if not rest:
        for at, width, total in parts:
            refs[0][:, at : at + width] = total
        return
    two, near, own = refs
    rows = two.shape[0]
    for k, (out, first) in enumerate(((two, 0), (near, 0), (near, rows), (own, 0))):

        @pl.when(step == k)
        def _(out=out, first=first):
            for at, width, total in parts:
                out[first : first + rows, at : at + width] = total


def weight_parts(pairs, places, first, more):
    piece = pairs[0][0][0].shape[1] // 8
    specs, args, columns = [], [], 0
    for lefts, rights in pairs:
        for left in lefts:
            specs.append(pl.BlockSpec((left.shape[0], piece), lambda i, places: (0, places[first + i])))
            args.append(left)
        for right, shape, at in rights:
            specs.append(pl.BlockSpec(shape, lambda i, places, at=at: at))
            args.append(right)
        columns += rights[0][1][1]
    if more is None:
        out_specs = pl.BlockSpec((piece, columns), lambda i, places: (i, 0))
        out_shape = like((4 * piece, columns), BF)
    else:
        specs.append(pl.BlockSpec((piece, columns), lambda i, places: (i, 0)))
        args.append(more)
        out_shape = [like((piece * n, columns), BF) for n in (1, 2, 1)]
        out_specs = [pl.BlockSpec(o.shape, lambda i, places: (0, 0)) for o in out_shape]
    return pl.pallas_call(
        functools.partial(weight_kernel, counts=[len(lefts) for lefts, _ in pairs], rest=more is not None),
        grid_spec=pltpu.PrefetchScalarGridSpec(num_scalar_prefetch=1, grid=(4,), in_specs=specs, out_specs=out_specs),
        out_shape=out_shape,
        compiler_params=pltpu.CompilerParams(vmem_limit_bytes=16 * MIB),
        cost_estimate=NO_COST,
        name="weight_parts",
    )(places, *args)


def piece_places():
    size = lax.axis_size("x")
    xi = lax.axis_index("x")

    def number(half, step):
        return half * size + (xi + step + size) % size

    def kept(core):
        way = 1 - 2 * core
        return [number(core, 2), number(core, way), number(1 - core, way), number(core, 0)]

    core = lax.axis_index("c")
    way = 1 - 2 * core
    last = [number(core, 0), number(1 - core, 0), number(core, -way), number(1 - core, -way)]
    last += [number(1 - core, way), number(core, way), number(core, 2), number(1 - core, 2)]
    return [jnp.stack(p).astype(jnp.int32) for p in (kept(1 - core) + kept(core), last)]


def holding(line, pairs):
    (lefts, rights), *more = pairs
    return [([line.hold(lefts[0]), *lefts[1:]], rights), *more]


class OverGroups:
    def __init__(self, places):
        self.places = places

    def send(self, line, pairs):
        self.pairs = pairs
        self.other = shifted(line.done(weight_parts(holding(line, pairs), self.places, 0, None)), "c", 1)

    def keep(self, line):
        line.wait(self.other)
        two, self.side, self.own = weight_parts(holding(line, self.pairs), self.places, 4, self.other)
        line.done(self.own)
        self.passed = across_back(two, "x")

    def near(self, line):
        line.wait(self.passed)
        shape = self.side.shape
        side = simple(near_kernel, [like(shape, BF)], [line.hold(self.side), self.passed], "near", 8)[0]
        self.come = across_back(line.done(side), "x")

    def half(self, line):
        line.wait(self.come)
        self.come = line.done(line.hold(self.come))
        self.swapped = shifted(self.come, "c", 1)

    def quarter(self, line):
        line.wait(self.swapped)
        args = [line.hold(self.own), self.come, self.swapped]
        self.mine = line.done(simple(quarter_kernel, [like(self.own.shape, BF)], args, "quarter", 8)[0])
        self.theirs = shifted(self.mine, "yh", 1)

    def whole(self, line):
        line.wait(self.theirs)
        self.mine = line.done(added(line.hold(self.mine), self.theirs))
        self.swapped = shifted(self.mine, "c", 1)

    def spread(self, line):
        line.wait(self.swapped)
        rows, width = self.mine.shape
        args = [line.hold(self.mine), self.swapped]
        self.both = line.done(simple(both_kernel, [like((2 * rows, width), BF)], args, "both", 8)[0])
        self.come = across_back(self.both, "x")

    def last(self, line):
        line.wait(self.come)
        upper = simple(upper_kernel, [like(self.mine.shape, BF)], [line.hold(self.come)], "upper", 6)[0]
        self.two = across_back(line.done(upper), "x")

    def swap(self, line):
        line.wait(self.two)
        come, two = line.hold(self.come), line.hold(self.two)
        self.moved = [shifted(come, "c", 1), shifted(two, "c", 1)]

    def pieces(self, line):
        line.wait(*self.moved)
        return [line.hold(self.both), self.come, self.moved[0], self.two, self.moved[1]]


def place_kernel(places, *refs, columns, turned, counts):
    step = pl.program_id(0)
    pieces, outs = refs[: len(counts)], refs[len(counts) :]
    first = 0
    for piece, count in zip(pieces, counts):

        @pl.when((step >= first) & (step < first + count))
        def _(piece=piece):
            at = 0
            for out, width, turn_it in zip(outs, columns, turned):
                value = piece[:, at : at + width].astype(F32)
                out[...] = value.T if turn_it else value
                at += width

        first += count


def placed(pieces, places, columns, turned):
    rows = min(p.shape[0] for p in pieces)
    counts = [p.shape[0] // rows for p in pieces]
    out_specs, out_shape, in_specs = [], [], []
    for width, turn_it in zip(columns, turned):
        if turn_it:
            out_specs.append(pl.BlockSpec((width, rows), lambda i, places: (0, places[i])))
            out_shape.append(jax.ShapeDtypeStruct((width, 8 * rows), F32))
        else:
            out_specs.append(pl.BlockSpec((rows, width), lambda i, places: (places[i], 0)))
            out_shape.append(jax.ShapeDtypeStruct((8 * rows, width), F32))
    first = 0
    for piece, count in zip(pieces, counts):
        in_specs.append(
            pl.BlockSpec((rows, piece.shape[1]), lambda i, places, f=first, n=count: (jnp.clip(i - f, 0, n - 1), 0))
        )
        first += count
    return pl.pallas_call(
        functools.partial(place_kernel, columns=columns, turned=turned, counts=counts),
        grid_spec=pltpu.PrefetchScalarGridSpec(
            num_scalar_prefetch=1, grid=(8,), in_specs=in_specs, out_specs=out_specs
        ),
        out_shape=out_shape,
        compiler_params=pltpu.CompilerParams(vmem_limit_bytes=16 * MIB),
        cost_estimate=NO_COST,
        name="placed",
    )(places, *pieces)


def local(
    tokens_in,
    cotangent,
    lengths,
    ln1_gain,
    ln1_bias,
    w_query,
    w_key,
    w_value,
    w_gate,
    w_out,
    ln2_gain,
    ln2_bias,
    w_up,
    b_up,
    w_down,
    b_down,
):
    rows = tokens_in.shape[0]
    half = rows * 4
    z_size = lax.axis_size("z")
    blocks = z_size * lax.axis_size("yl")
    zi = lax.axis_index("z")
    yi = lax.axis_index("yl")
    ends = jnp.cumsum(lengths[0])
    marks = [((yi + dy) % 2) * z_size + (zi + dz) % z_size for dz, dy in ORDER] + [ends[0], ends[1]]
    marks = jnp.stack([m.astype(jnp.int32) for m in marks])
    decay = jnp.log1p(-jnp.exp2(-5.0 - lax.axis_index(MP).astype(F32)))[None]
    tables = angle_tables(rows, blocks)
    places, final = piece_places()
    weights = (w_query, w_key, w_value, w_gate)
    heads_weights = tuple(in_hbm(w) for w in weights)
    gain_one, bias_one, gain_two, bias_two = (v[None, :] for v in (ln1_gain, ln1_bias, ln2_gain, ln2_bias))
    square = (half, DV)
    line = Line()

    xg = Gather(line.done(norm(tokens_in, gain_one, bias_one)))
    cg = LateGather(line.hold(cotangent))
    line.done(marks)
    xg.second(line)
    got = xg.got
    line.wait(got[2, 0], cg.got[0, 1])
    cg.sides(line)
    x_a, q_a, k_a, v_a, gate_a = heads(
        marks, [line.hold(got[0, 0]), got[1, 0], got[-1, 0], got[0, 1]], heads_weights, tables, 0
    )
    line.done(q_a)
    line.wait(got[1, 1], got[-1, 1], got[2, 1])
    x_b, q_b, k_b, v_b, gate_b = heads(
        marks, [line.hold(got[2, 0])] + xg.wave(WAVE_B[1:]), heads_weights, tables, 4
    )
    line.done(q_b)
    ks, vs = (k_a, k_b), (v_a, v_b)
    ret_b, gated_b, part_b = retain(marks, decay, WAVE_B, q_b, ks, vs, gate_b, w_out)
    line.done(gated_b)
    cot = cg.got
    line.wait(cot[1, 0], cot[-1, 0], cot[1, 1], cot[-1, 1])
    ret_a, gated_a, part_a = retain(marks, decay, WAVE_A, line.hold(q_a), ks, vs, gate_a, w_out)
    line.done(gated_a)
    rs = Scatter({**part_a, **part_b})
    rs.relay(line)
    rs.side(line)
    cg.second(line)
    rs.near(line)
    cot_a, dh_a = hidden_grad([line.hold(cot[0, 0])] + cg.wave(WAVE_A[1:]), w_down)
    line.done(dh_a)
    line.wait(cot[2, 0])
    cg.third(line)
    first, *others = rs.terms()
    line.wait(*others)
    middle, normed_two = middle_norm(tokens_in, [line.hold(first), *others], gain_two, bias_two)

    ng = Gather(line.done(normed_two))
    line.wait(cot[2, 1])
    cot_b, dh_b = hidden_grad([line.hold(cot[2, 0])] + cg.wave(WAVE_B[1:]), w_down)
    line.done(dh_b)
    ng.second(line)
    got = ng.got
    line.wait(got[2, 0])
    n_a, hid_a, dpre_a, bsum_a, part_a = feed(
        WAVE_A, [line.hold(got[0, 0]), got[1, 0], got[-1, 0], got[0, 1]], w_up, b_up[None, :], dh_a
    )
    line.done(bsum_a)
    line.wait(got[1, 1], got[-1, 1], got[2, 1])
    n_b, hid_b, dpre_b, bsum_b, part_b = feed(
        WAVE_B, [line.hold(got[2, 0])] + ng.wave(WAVE_B[1:]), w_up, b_up[None, :], dh_b
    )
    line.done(bsum_b)
    rs = Scatter({**part_a, **part_b})
    out_b = feed_out(WAVE_B, line.hold(hid_b), w_down)
    line.done(out_b[2, 1])
    out_a = feed_out(WAVE_A, line.hold(hid_a), w_down)
    line.done(out_a[0, 1])
    rs.relay(line)
    rs.side(line)
    feed_sums = OverGroups(places)
    feed_sums.send(
        line,
        [
            ([n_a, n_b], [(dpre_a, dpre_a.shape, (0, 0)), (dpre_b, dpre_b.shape, (0, 0))]),
            ([cot_a, cot_b], [(hid_a, hid_a.shape, (0, 0)), (hid_b, hid_b.shape, (0, 0))]),
        ],
    )
    rs.near(line)
    feed_sums.keep(line)
    first, *others = rs.terms()
    line.wait(*others)
    grad_middle, branch, early = middle_back(middle, cotangent, [line.hold(first), *others], gain_two)

    bg = Gather(line.done(branch))
    feed_sums.near(line)
    bg.second(line)
    got = bg.got
    line.wait(got[2, 0])
    br_a, dret_a, dgate_a = gate_back(
        [line.hold(got[0, 0]), got[1, 0], got[-1, 0], got[0, 1]], w_out, ret_a, gate_a
    )
    line.done(dret_a)
    feed_sums.half(line)
    feed_sums.quarter(line)
    line.wait(got[1, 1], got[-1, 1], got[2, 1])
    br_b, dret_b, dgate_b = gate_back([line.hold(got[2, 0])] + bg.wave(WAVE_B[1:]), w_out, ret_b, gate_b)
    line.done(dret_b)
    gate_sums = OverGroups(places)
    gate_sums.send(
        line,
        [
            ([x_a, x_b], [(dgate_a, square, (0, 0)), (dgate_b, square, (0, 0))]),
            ([br_a, br_b], [(gated_a, square, (0, 0)), (gated_b, square, (0, 0))]),
        ],
    )
    dqkv_a, dqkv_b = retain_back(marks, decay, (q_a, q_b), ks, vs, (line.hold(dret_a), dret_b), tables)
    line.done(dqkv_b)
    gate_sums.keep(line)
    feed_sums.whole(line)
    part_b = heads_back(WAVE_B, line.hold(dqkv_b), dgate_b, weights)
    line.done(part_b[2, 1])
    part_a = heads_back(WAVE_A, line.hold(dqkv_a), dgate_a, weights)
    line.done(part_a[0, 1])
    rs = Scatter({**part_a, **part_b})
    gate_sums.near(line)
    head_sums = OverGroups(places)
    head_sums.send(line, [([x_a, x_b], [(dqkv_a, dqkv_a.shape, (0, 0)), (dqkv_b, dqkv_b.shape, (0, 0))])])
    rs.relay(line)
    rs.side(line)
    head_sums.keep(line)
    gate_sums.half(line)
    gate_sums.quarter(line)
    rs.near(line)
    head_sums.near(line)
    line.wait(rs.other)
    first, *others = rs.terms()
    line.wait(*others)
    grad_x, late = input_back(tokens_in, grad_middle, [line.hold(first), *others], gain_one)
    line.done(late)
    sums = Summed(line.done(jnp.concatenate([late, early], 0)), ("z", "yl"))
    gate_sums.whole(line)
    gate_sums.spread(line)
    sums.step(line)
    head_sums.half(line)
    head_sums.quarter(line)
    sums.step(line)
    sums.step(line)
    gate_sums.last(line)
    feed_sums.spread(line)
    head_sums.whole(line)
    head_sums.spread(line)
    sums.step(line)
    wide = jnp.pad(bsum_a + bsum_b, ((0, 0), (0, early.shape[1] - bsum_a.shape[1])))
    sums = Summed(line.done(jnp.concatenate([line.hold(sums.value), wide], 0)), ("c", "yh", "x"))
    sums.step(line)
    out_rs = Scatter({**out_a, **{p: line.hold(v) for p, v in out_b.items()}})
    gate_sums.swap(line)
    sums.step(line)
    gate_pieces = [in_hbm(p) for p in gate_sums.pieces(line)]
    grad_gate, grad_out = placed(gate_pieces, final, (DV, DV), (False, True))
    line.done(grad_gate)
    feed_sums.last(line)
    head_sums.last(line)
    out_rs.relay(line)
    out_rs.side(line)
    feed_sums.swap(line)
    grad_up, grad_down = placed(feed_sums.pieces(line), final, (w_up.shape[1], w_down.shape[0]), (False, True))
    line.done(grad_up)
    out_rs.near(line)
    sums.step(line)
    head_sums.swap(line)
    sums.step(line)
    grad_query, grad_key, grad_value = placed(head_sums.pieces(line), final, (DK, DK, DV), (False, False, False))
    sums.step(line)
    line.wait(grad_query)
    sums = sums.value
    b_up_sum = sums[5, : bsum_a.shape[1]]
    first, *others = out_rs.terms()
    result = middle + plus(line.hold(first), *others) + b_down
    return (
        result.astype(BF),
        grad_x,
        sums[0],
        sums[1],
        grad_query,
        grad_key,
        grad_value,
        grad_gate,
        grad_out,
        sums[2],
        sums[3],
        grad_up,
        b_up_sum,
        grad_down,
        sums[4],
    )


def solution(mesh):
    split = Mesh(mesh.devices.reshape(4, 2, 2, 2, 4), AXES)
    rows = P(AXES, None)
    cols = P(None, MP)
    mp_rows = P(MP, None)
    return jax.shard_map(
        local,
        mesh=split,
        in_specs=(
            rows, rows, P(DP, None), P(), P(), cols, cols, cols, cols, mp_rows, P(), P(), cols, P(MP), mp_rows, P(),
        ),
        out_specs=(
            rows, rows, P(), P(), cols, cols, cols, cols, mp_rows, P(), P(), cols, P(MP), mp_rows, P(),
        ),
        check_vma=False,
    )
```
